256 devices in a mesh: dp: 16 (over z, core), feat: 16 (over x, y).
Axes of the slice: x: 4, y: 4, z: 8, core: 2. Of those that a mesh axis runs over, the one named last changes fastest.
Arguments:
- design: bfloat16 [32768, 16384], P('dp', 'feat'), may hold values from -0.3314563 to 0.3314563
- sketch: bfloat16 [1536, 32768], P(None, 'dp'), may hold values from -0.15625 to 0.15625
- targets: float32 [64, 32768], P(None, 'dp'), may hold values from -6 to 6
Outputs:
- solution: float32 [64, 16384], P(None, 'feat')
- residual_ratio: float32 [64], replicated
The draws below stay inside these ranges and needn't reach their ends.
All inputs are finite; a program needn't handle non-finite values.
Results may differ from the reference program's by a relative error of at most 0.0003.
Values sent between devices are 32-bit elements; how exact they have to be, the bound alone decides.
A program may use at most 128 MiB of HBM per device.

```python
import math
import jax
import jax.numpy as jnp
from jax import lax

COLBLK = 1024
K = 64
SK = 1536
ITERS = 2
N = 16384
ROWS = 32768


def draw_design(key, part):
    key = jax.random.fold_in(key, 11)
    key_base, key_scale = jax.random.split(key, 2)
    scales = jnp.exp(jax.random.uniform(key_scale, (1, N), jnp.float32) * math.log(10.0))
    base_vals = jnp.clip(jax.random.normal(key_base, (ROWS, N), jnp.float32), -6.0, 6.0)
    return (base_vals * scales * ROWS ** (-0.5)).astype(jnp.bfloat16)


def block_levels(own_key, shape, pieces, smallest, largest):
    def one(axis_at, blocks):
        heights = jax.random.uniform(jax.random.fold_in(jax.random.fold_in(own_key, 6), axis_at), (blocks,), jnp.float32, smallest / len(pieces), largest / len(pieces))
        return jnp.repeat(jnp.exp(heights), shape[axis_at] // blocks).reshape((-1,) + (1,) * (len(shape) - axis_at - 1))

    gain = one(*pieces[0])
    for cut in pieces[1:]:
        gain = gain * one(*cut)
    return gain


def scatter_about(rng, shape, deviation, bound, shards=(), held_as=jnp.bfloat16):
    loudness = block_levels(rng, shape, shards, -0.22, 0.18) if shards else 1.0
    drawn = jax.random.normal(rng, shape, jnp.float32) * deviation * loudness
    return jnp.minimum(jnp.maximum(drawn, -bound), bound).astype(held_as)


def setup_inputs(seed: int = 0) -> dict:
    key_of = jax.random.split(jax.random.key(seed), 4)
    design = draw_design(jax.random.fold_in(key_of[3], 71), 0)
    sketch = scatter_about(key_of[1], (SK, ROWS), SK ** -0.5, 0.15625, ((1, 16),))
    targets = scatter_about(key_of[2], (K, ROWS), 1.0, 6.0, ((1, 16),), jnp.float32)
    return {"design": design, "sketch": sketch, "targets": targets}


NORM_EPS = 1e-06
TOP_PRECISION = lax.Precision.HIGHEST

def reference(design, sketch, targets):
    blocks = N // COLBLK
    sketch_wide = sketch.astype(jnp.float32)
    block_ids = jnp.arange(blocks, dtype=jnp.int32)

    def column_block(block_idx):
        return lax.dynamic_slice_in_dim(design, block_idx * COLBLK, COLBLK, 1).astype(jnp.float32)

    def factor(block_idx):
        sketched = jnp.dot(sketch_wide, column_block(block_idx), precision=TOP_PRECISION)
        gram_mat = jnp.dot(sketched.T, sketched, precision=TOP_PRECISION)
        return jnp.linalg.cholesky(gram_mat)
    lowers = lax.map(factor, block_ids)

    def to_blocks(vec):
        return vec.reshape(K, blocks, COLBLK).transpose(1, 0, 2)

    def from_blocks(vec_blocks):
        return vec_blocks.transpose(1, 0, 2).reshape(K, blocks * COLBLK)

    def precondition(vec):
        return from_blocks(lax.linalg.triangular_solve(lowers, to_blocks(vec), left_side=False, lower=True))

    def adjoint_pre(vec):
        return from_blocks(lax.linalg.triangular_solve(lowers, to_blocks(vec), left_side=False, lower=True, transpose_a=True))

    def forward(vec):
        pre_blocks = to_blocks(precondition(vec))

        def accumulate(running, block_idx):
            return (running + jnp.dot(pre_blocks[block_idx], column_block(block_idx).T, precision=TOP_PRECISION), None)
        image_rows, _ = lax.scan(accumulate, jnp.zeros((K, ROWS), jnp.float32), block_ids)
        return image_rows

    def adjoint(vec):
        columns = lax.map(lambda block_idx: jnp.dot(vec, column_block(block_idx), precision=TOP_PRECISION), block_ids)
        return adjoint_pre(columns.transpose(1, 0, 2).reshape(K, blocks * COLBLK))
    beta_norm = jnp.sqrt(lax.optimization_barrier(jnp.sum(targets * targets, axis=1)) + NORM_EPS)
    beta_first = beta_norm
    left_vec = targets / beta_norm[:, None]
    right_raw = adjoint(left_vec)
    alpha_norm = jnp.sqrt(lax.optimization_barrier(jnp.sum(right_raw * right_raw, axis=1)) + NORM_EPS)
    right_vec = right_raw / alpha_norm[:, None]
    search_dir = right_vec
    coords = jnp.zeros((K, N), jnp.float32)
    rho_bar = alpha_norm
    phi_bar = beta_norm
    for step_idx in range(ITERS):
        left_raw = forward(right_vec) - alpha_norm[:, None] * left_vec
        beta_norm = jnp.sqrt(lax.optimization_barrier(jnp.sum(left_raw * left_raw, axis=1)) + NORM_EPS)
        left_vec = left_raw / beta_norm[:, None]
        rho_full = jnp.sqrt(rho_bar * rho_bar + beta_norm * beta_norm)
        cosine = rho_bar / rho_full
        sine_val = beta_norm / rho_full
        phi_step = cosine * phi_bar
        phi_bar = sine_val * phi_bar
        coords = coords + (phi_step / rho_full)[:, None] * search_dir
        if step_idx + 1 < ITERS:
            right_raw = adjoint(left_vec) - beta_norm[:, None] * right_vec
            alpha_norm = jnp.sqrt(lax.optimization_barrier(jnp.sum(right_raw * right_raw, axis=1)) + NORM_EPS)
            right_vec = right_raw / alpha_norm[:, None]
            theta_val = sine_val * alpha_norm
            rho_bar = -cosine * alpha_norm
            search_dir = right_vec - (theta_val / rho_full)[:, None] * search_dir
    return (precondition(coords), phi_bar / beta_first)
```

```python
import functools

import jax
import jax.numpy as jnp
from jax import lax
from jax.experimental import pallas as pl
from jax.experimental.pallas import tpu as pltpu
from jax.sharding import PartitionSpec as P

ITERS = 2
NORM_EPS = 1e-06
TOP_PRECISION = lax.Precision.HIGHEST
F32 = jnp.float32
BF16 = jnp.bfloat16
MESH = pl.DeviceIdType.MESH
NN = ((1,), (0,))
NT = ((1,), (1,))
SUB = 8
LANES = 128
BLK = 128
MIB = 2**20


def split3(x):
    high = x.astype(BF16)
    rest = x - high.astype(F32)
    mid = rest.astype(BF16)
    return high, mid, (rest - mid.astype(F32)).astype(BF16)


def dot32(a, b, dims):
    return lax.dot_general(a, b, (dims, ((), ())), preferred_element_type=F32)


def lane_splat(x, c):
    return jnp.broadcast_to(x[:, c : c + 1], x.shape)


def row_splat(x, r):
    return jnp.broadcast_to(x[r : r + 1, :], x.shape)


def tree_sum(terms):
    while len(terms) > 1:
        terms = [
            terms[i] + terms[i + 1] if i + 1 < len(terms) else terms[i]
            for i in range(0, len(terms), 2)
        ]
    return terms[0]


def factor_block(d_ref, w_ref):
    n = BLK // SUB
    rid = lax.broadcasted_iota(jnp.int32, (SUB, BLK), 0)
    lid = lax.broadcasted_iota(jnp.int32, (SUB, BLK), 1)
    a = [d_ref[SUB * i : SUB * i + SUB, :] for i in range(n)]
    w = [jnp.where(lid == rid + SUB * i, 1.0, 0.0) for i in range(n)]
    for g in range(n):
        cols = [lane_splat(a[g], SUB * g + c) for c in range(SUB)]
        rows_a, rows_w, low_w = a[g], w[g], w[g]
        inv_pivots = jnp.zeros((SUB, BLK), F32)
        for k in range(SUB):
            inv = 1.0 / row_splat(cols[k], k)
            mult = jnp.where(rid == k, 0.0, cols[k]) * inv
            for j in range(k + 1, SUB):
                cols[j] = cols[j] - mult * row_splat(cols[j], k)
            rows_a = rows_a - mult * row_splat(rows_a, k)
            rows_w = rows_w - mult * row_splat(rows_w, k)
            low_w = low_w - jnp.where(rid > k, mult, 0.0) * row_splat(low_w, k)
            inv_pivots = jnp.where(rid == k, inv, inv_pivots)
        rows_a = rows_a * inv_pivots
        rows_w = rows_w * inv_pivots
        w_ref[SUB * g : SUB * g + SUB, :] = low_w * jnp.sqrt(inv_pivots)
        if g < n - 1:
            splat_a = [row_splat(rows_a, c) for c in range(SUB)]
            splat_w = [row_splat(rows_w, c) for c in range(SUB)]
            for i in range(g + 1, n):
                p = [lane_splat(a[i], SUB * g + c) for c in range(SUB)]
                a[i] = a[i] - tree_sum([p[c] * splat_a[c] for c in range(SUB)])
                w[i] = w[i] - tree_sum([p[c] * splat_w[c] for c in range(SUB)])


def factor_kernel(g_in, w_ref, g_ref, d_ref, wk_ref, x_ref, y_ref, z_ref):
    size = g_ref.shape[0]
    blocks = size // BLK
    g_ref[...] = g_in[...]
    w_ref[...] = jnp.zeros_like(w_ref)

    def step(k, carry):
        at = pl.multiple_of(k * BLK, BLK)
        d_ref[...] = g_ref[pl.ds(at, BLK), pl.ds(at, BLK)]
        factor_block(d_ref, wk_ref)
        for this in range(blocks):

            @pl.when(k == this)
            def _():
                lo = this * BLK
                nxt = lo + BLK
                wk = wk_ref[...]
                wh, wm, wl = split3(wk)
                if this > 0:
                    ah, am, al = split3(w_ref[lo:nxt, 0:lo])
                    row = dot32(
                        jnp.concatenate([wh, wh, wm, wh, wm, wl], axis=1),
                        jnp.concatenate([ah, am, ah, al, am, ah], axis=0),
                        NN,
                    )
                    w_ref[lo:nxt, 0:lo] = row
                    rh, rm, rl = split3(row)
                    for t, part in enumerate([rh, rm, rh, rl, rm, rh]):
                        z_ref[t * BLK : (t + 1) * BLK, 0:lo] = part
                w_ref[lo:nxt, lo:nxt] = wk
                for t, part in enumerate([wh, wm, wh, wl, wm, wh]):
                    z_ref[t * BLK : (t + 1) * BLK, lo:nxt] = part
                if nxt < size:
                    gh, gm, gl = split3(g_ref[nxt:, lo:nxt])
                    panel = dot32(
                        jnp.concatenate([gh, gh, gm, gh, gm, gl], axis=1),
                        jnp.concatenate([wh, wm, wh, wl, wm, wh], axis=1),
                        NT,
                    )
                    ph, pm, pw = split3(panel)
                    for t, part in enumerate([ph, ph, pm, ph, pm, pw]):
                        x_ref[nxt:, t * BLK : (t + 1) * BLK] = part
                    for t, part in enumerate([ph, pm, ph, pw, pm, ph]):
                        y_ref[nxt:, t * BLK : (t + 1) * BLK] = part
                    j = nxt
                    while j < size:
                        wide = 2 * BLK if j % (2 * BLK) == 0 else BLK
                        g_ref[j:, j : j + wide] -= dot32(x_ref[j:, :], y_ref[j : j + wide, :], NT)
                        j += wide
                    w_ref[nxt:, 0:nxt] -= dot32(x_ref[nxt:, :], z_ref[:, 0:nxt], NN)

        return carry

    lax.fori_loop(0, blocks, step, 0)


def inverse_factor(gram):
    size = gram.shape[0]
    return pl.pallas_call(
        factor_kernel,
        out_shape=jax.ShapeDtypeStruct((size, size), F32),
        in_specs=[pl.BlockSpec(memory_space=pltpu.VMEM)],
        out_specs=pl.BlockSpec(memory_space=pltpu.VMEM),
        scratch_shapes=[
            pltpu.VMEM((size, size), F32),
            pltpu.VMEM((BLK, BLK), F32),
            pltpu.VMEM((BLK, BLK), F32),
            pltpu.VMEM((size, 6 * BLK), BF16),
            pltpu.VMEM((size, 6 * BLK), BF16),
            pltpu.VMEM((6 * BLK, size), BF16),
        ],
        compiler_params=pltpu.CompilerParams(vmem_limit_bytes=48 * MIB),
    )(gram)


class Group:
    def __init__(self, axis, n):
        self.axis, self.n = axis, n
        self.me = lax.axis_index(axis)

    def peer(self, t):
        return lax.rem(self.me + t, self.n)

    def source(self, t):
        return lax.rem(self.me + self.n - t, self.n)

    def each(self, fn):
        def step(t, carry):
            fn(t)
            return carry

        lax.fori_loop(1, self.n, step, 0)

    def copy(self, src, dst, sems, t):
        return pltpu.make_async_remote_copy(
            src_ref=src,
            dst_ref=dst,
            send_sem=sems.at[0, t - 1],
            recv_sem=sems.at[1, t - 1],
            device_id={self.axis: self.peer(t)},
            device_id_type=MESH,
        )

    def greet(self, barrier):
        self.each(
            lambda t: pl.semaphore_signal(
                barrier, inc=1, device_id={self.axis: self.peer(t)}, device_id_type=MESH
            )
        )

    def scatter_sum(self, stage, recv, sems):
        self.each(lambda t: self.copy(stage.at[self.peer(t)], recv.at[t - 1], sems, t).start())
        self.each(lambda t: self.copy(stage.at[self.peer(t)], recv.at[t - 1], sems, t).wait())
        return tree_sum([stage[self.me]] + [recv[t] for t in range(self.n - 1)])

    def gather(self, value, out, sems):
        out[self.me] = value
        self.each(lambda t: self.copy(out.at[self.me], out.at[self.me], sems, t).start())

        def wait(t):
            src = self.source(t)
            self.copy(out.at[src], out.at[src], sems, t).wait_recv()
            self.copy(out.at[self.me], out.at[self.me], sems, t).wait_send()

        self.each(wait)


def lane_partial(x):
    return tree_sum(
        [x[:, i : i + LANES] * x[:, i : i + LANES] for i in range(0, x.shape[1], LANES)]
    )


def norm_of(lanes):
    return jnp.sqrt(jnp.sum(lanes, axis=1, keepdims=True) + NORM_EPS)


def put_slices(stage, value, extra):
    n, _, wide = stage.shape
    halves = n * SUB // value.shape[0]
    part = value.shape[1] // halves
    for d in range(n):
        r, h = SUB * (d // halves), part * (d % halves)
        stage[d, :, 0:part] = value[r : r + SUB, h : h + part]
        if extra is not None:
            stage[d, :, part:wide] = extra[r : r + SUB, :]


def take_slices(out, k, part):
    n = out.shape[0]
    halves = n * SUB // k
    value = jnp.concatenate(
        [
            jnp.concatenate([out[g * halves + h, :, 0:part] for h in range(halves)], axis=1)
            for g in range(n // halves)
        ],
        axis=0,
    )
    extra = jnp.concatenate(
        [out[g * halves, :, part : part + LANES] for g in range(n // halves)], axis=0
    )
    return value, extra


def times_exact(x, mat, dims):
    k = x.shape[0]
    both = dot32(jnp.concatenate(split3(x), axis=0), mat, dims)
    return both[0:k] + (both[k : 2 * k] + both[2 * k : 3 * k])


def times_split(x, parts, dims):
    k = x.shape[0]
    high, mid, low = split3(x)
    mh, mm, ml = parts
    a = dot32(jnp.concatenate([high, mid, low], axis=0), mh, dims)
    b = dot32(jnp.concatenate([high, mid], axis=0), mm, dims)
    c = dot32(high, ml, dims)
    return a[0:k] + ((a[k : 2 * k] + b[0:k]) + ((a[2 * k : 3 * k] + b[k : 2 * k]) + c))


def lsqr_kernel(
    n_dp,
    n_feat,
    a_ref,
    t_ref,
    w_ref,
    sol_ref,
    ratio_ref,
    wh,
    wm,
    wl,
    u_ref,
    vec_ref,
    img_ref,
    d_stage,
    d_recv,
    d_out,
    d_stage2,
    d_recv2,
    d_out2,
    f_stage,
    f_recv,
    f_out,
    f_stage2,
    f_recv2,
    small_dp,
    small_feat,
    dp_sems,
    feat_sems,
):
    dp = Group("dp", n_dp)
    feat = Group("feat", n_feat)
    k, rows = t_ref.shape
    cols = a_ref.shape[1]
    f_halves = n_feat * SUB // k
    f_part = rows // f_halves
    d_part = cols // (n_dp * SUB // k)

    barrier = pltpu.get_barrier_semaphore()
    dp.greet(barrier)
    feat.greet(barrier)
    pl.semaphore_wait(barrier, n_dp + n_feat - 2)

    def preconditioned(vec):
        return times_split(vec, (wh[...], wm[...], wl[...]), NN)

    def adjoint_pre(vec):
        return times_split(vec, (wh[...], wm[...], wl[...]), NT)

    targets = t_ref[...]
    put_slices(d_stage, times_exact(targets, a_ref[...], NN), lane_partial(targets))
    total = dp.scatter_sum(d_stage, d_recv, dp_sems.at[0])
    dp.gather(total, d_out, dp_sems.at[1])
    h, m, l = split3(w_ref[...])
    wh[...] = h
    wm[...] = m
    wl[...] = l
    adj, squares = take_slices(d_out, k, d_part)
    beta_first = norm_of(squares)
    u_ref[...] = targets / beta_first

    v_raw = adjoint_pre(adj / beta_first)
    y_raw = preconditioned(v_raw)
    put_slices(f_stage, times_exact(y_raw, a_ref[...], NT), lane_partial(v_raw))
    total = feat.scatter_sum(f_stage, f_recv, feat_sems.at[0])
    feat.gather(total, f_out, feat_sems.at[1])
    image, squares = take_slices(f_out, k, f_part)
    alpha = norm_of(squares)
    v = v_raw / alpha
    w = y_raw / alpha
    rho_bar = alpha
    phi_bar = beta_first

    u_raw = image / alpha - alpha * u_ref[...]
    put_slices(d_stage2, times_exact(u_raw, a_ref[...], NN), lane_partial(u_raw))
    total = dp.scatter_sum(d_stage2, d_recv2, dp_sems.at[2])
    dp.gather(total, d_out2, dp_sems.at[3])
    adj, squares = take_slices(d_out2, k, d_part)
    beta = norm_of(squares)
    u_ref[...] = u_raw / beta
    rho = jnp.sqrt(rho_bar * rho_bar + beta * beta)
    cosine = rho_bar / rho
    sine = beta / rho
    phi = cosine * phi_bar
    phi_bar = sine * phi_bar
    coords = (phi / rho) * w
    v_raw = adjoint_pre(adj / beta) - beta * v
    y_raw = preconditioned(v_raw)

    put_slices(f_stage2, times_exact(y_raw, a_ref[...], NT), lane_partial(v_raw))
    put_slices(img_ref, u_ref[...], None)
    total = feat.scatter_sum(f_stage2, f_recv2, feat_sems.at[2])
    squares = total[:, f_part:]
    alpha = norm_of(squares)
    left = total[:, 0:f_part] / alpha - alpha * img_ref[feat.me]
    dp.gather(lane_partial(left), small_dp, dp_sems.at[4])
    norms = tree_sum([small_dp[i] for i in range(n_dp)])
    feat.gather(jnp.concatenate([norms, squares], axis=1), small_feat, feat_sems.at[3])
    groups = n_feat // f_halves
    norms = jnp.concatenate(
        [
            tree_sum([small_feat[g * f_halves + i, :, 0:LANES] for i in range(f_halves)])
            for g in range(groups)
        ],
        axis=0,
    )
    squares = jnp.concatenate([small_feat[g * f_halves, :, LANES:] for g in range(groups)], axis=0)
    alpha = norm_of(squares)
    theta = sine * alpha
    rho_bar = -cosine * alpha
    w = y_raw / alpha - (theta / rho) * w
    beta = norm_of(norms)
    rho = jnp.sqrt(rho_bar * rho_bar + beta * beta)
    cosine = rho_bar / rho
    sine = beta / rho
    phi = cosine * phi_bar
    phi_bar = sine * phi_bar
    sol_ref[...] = coords + (phi / rho) * w
    ratio_ref[...] = jnp.broadcast_to(phi_bar / beta_first, ratio_ref.shape)


def lsqr(design, targets, winv, n_dp, n_feat):
    rows, cols = design.shape
    k = targets.shape[0]
    d_wide = cols * k // (n_dp * SUB) + LANES
    f_wide = rows * k // (n_feat * SUB) + LANES
    vmem = pl.BlockSpec(memory_space=pltpu.VMEM)
    d_bufs = [
        pltpu.VMEM((n_dp, SUB, d_wide), F32),
        pltpu.VMEM((n_dp - 1, SUB, d_wide), F32),
        pltpu.VMEM((n_dp, SUB, d_wide), F32),
    ]
    f_bufs = [
        pltpu.VMEM((n_feat, SUB, f_wide), F32),
        pltpu.VMEM((n_feat - 1, SUB, f_wide), F32),
        pltpu.VMEM((n_feat, SUB, f_wide), F32),
    ]
    return pl.pallas_call(
        functools.partial(lsqr_kernel, n_dp, n_feat),
        out_shape=(
            jax.ShapeDtypeStruct((k, cols), F32),
            jax.ShapeDtypeStruct((k, LANES), F32),
        ),
        in_specs=[vmem] * 3,
        out_specs=(vmem, vmem),
        scratch_shapes=[pltpu.VMEM((cols, cols), BF16)] * 3
        + [
            pltpu.VMEM((k, rows), F32),
            pltpu.VMEM((k, cols), F32),
            pltpu.VMEM((n_feat, SUB, f_wide - LANES), F32),
        ]
        + d_bufs
        + d_bufs
        + f_bufs
        + f_bufs[:2]
        + [
            pltpu.VMEM((n_dp, SUB, LANES), F32),
            pltpu.VMEM((n_feat, SUB, 2 * LANES), F32),
            pltpu.SemaphoreType.DMA((5, 2, n_dp - 1)),
            pltpu.SemaphoreType.DMA((4, 2, n_feat - 1)),
        ],
        compiler_params=pltpu.CompilerParams(
            collective_id=0, has_side_effects=True, vmem_limit_bytes=56 * MIB
        ),
    )(design, targets, winv)


def body(n_dp, n_feat, design, sketch, targets):
    sketched = lax.psum_scatter(
        jnp.dot(sketch, design, preferred_element_type=F32),
        "dp",
        scatter_dimension=0,
        tiled=True,
    )
    local_gram = jnp.dot(
        sketched.T, sketched, precision=TOP_PRECISION, preferred_element_type=F32
    )
    winv = inverse_factor(lax.psum(local_gram, "dp"))
    sol, ratio = lsqr(design, targets, winv, n_dp, n_feat)
    return sol, ratio[:, 0]


def solution(mesh):
    return jax.shard_map(
        functools.partial(body, mesh.shape["dp"], mesh.shape["feat"]),
        mesh=mesh,
        in_specs=(P("dp", "feat"), P(None, "dp"), P(None, "dp")),
        out_specs=(P(None, "feat"), P()),
        check_vma=False,
    )
```

```python
import functools

import jax
import jax.numpy as jnp
from jax import lax
from jax.experimental import pallas as pl
from jax.experimental.pallas import tpu as pltpu
from jax.sharding import PartitionSpec as P

NORM_EPS = 1e-06
F32 = jnp.float32
BF16 = jnp.bfloat16
MESH = pl.DeviceIdType.MESH
NN = ((1,), (0,))
NT = ((1,), (1,))
SUB = 8
LANES = 128
BLK = 128
MIB = 2**20


def split3(x):
    high = x.astype(BF16)
    rest = x - high.astype(F32)
    mid = rest.astype(BF16)
    return high, mid, (rest - mid.astype(F32)).astype(BF16)


def dot32(a, b, dims):
    return lax.dot_general(a, b, (dims, ((), ())), preferred_element_type=F32)


def lane_splat(x, c):
    return jnp.broadcast_to(x[:, c : c + 1], x.shape)


def row_splat(x, r):
    return jnp.broadcast_to(x[r : r + 1, :], x.shape)


def tree_sum(terms):
    while len(terms) > 1:
        terms = [
            terms[i] + terms[i + 1] if i + 1 < len(terms) else terms[i]
            for i in range(0, len(terms), 2)
        ]
    return terms[0]


def factor_block(d_ref, w_ref):
    n = BLK // SUB
    rid = lax.broadcasted_iota(jnp.int32, (SUB, BLK), 0)
    lid = lax.broadcasted_iota(jnp.int32, (SUB, BLK), 1)
    a = [d_ref[SUB * i : SUB * i + SUB, :] for i in range(n)]
    w = [jnp.where(lid == rid + SUB * i, 1.0, 0.0) for i in range(n)]
    for g in range(n):
        cols = [lane_splat(a[g], SUB * g + c) for c in range(SUB)]
        rows_a, rows_w, low_w = a[g], w[g], w[g]
        inv_pivots = jnp.zeros((SUB, BLK), F32)
        for k in range(SUB):
            inv = 1.0 / row_splat(cols[k], k)
            mult = jnp.where(rid == k, 0.0, cols[k]) * inv
            for j in range(k + 1, SUB):
                cols[j] = cols[j] - mult * row_splat(cols[j], k)
            rows_a = rows_a - mult * row_splat(rows_a, k)
            rows_w = rows_w - mult * row_splat(rows_w, k)
            low_w = low_w - jnp.where(rid > k, mult, 0.0) * row_splat(low_w, k)
            inv_pivots = jnp.where(rid == k, inv, inv_pivots)
        rows_a = rows_a * inv_pivots
        rows_w = rows_w * inv_pivots
        w_ref[SUB * g : SUB * g + SUB, :] = low_w * jnp.sqrt(inv_pivots)
        if g < n - 1:
            splat_a = [row_splat(rows_a, c) for c in range(SUB)]
            splat_w = [row_splat(rows_w, c) for c in range(SUB)]
            for i in range(g + 1, n):
                p = [lane_splat(a[i], SUB * g + c) for c in range(SUB)]
                a[i] = a[i] - tree_sum([p[c] * splat_a[c] for c in range(SUB)])
                w[i] = w[i] - tree_sum([p[c] * splat_w[c] for c in range(SUB)])


def factor(g_ref, w_ref, d_ref, wk_ref, x_ref, y_ref, z_ref, between):
    size = g_ref.shape[0]
    blocks = size // BLK
    depth = 6 * BLK
    w_ref[...] = jnp.zeros_like(w_ref)

    def step(k, carry):
        at = pl.multiple_of(k * BLK, BLK)
        d_ref[...] = g_ref[pl.ds(at, BLK), pl.ds(at, BLK)]
        factor_block(d_ref, wk_ref)
        for this in range(blocks):

            @pl.when(k == this)
            def _():
                if this == 2:
                    between()
                lo = this * BLK
                nxt = lo + BLK
                wk = wk_ref[...]
                wh, wm, wl = split3(wk)
                if this > 0:
                    ah, am, al = split3(w_ref[lo:nxt, 0:lo])
                    row = dot32(
                        jnp.concatenate([wh, wh, wm, wh, wm, wl], axis=1),
                        jnp.concatenate([ah, am, ah, al, am, ah], axis=0),
                        NN,
                    )
                    w_ref[lo:nxt, 0:lo] = row
                    rh, rm, rl = split3(row)
                    for t, part in enumerate([rh, rm, rh, rl, rm, rh]):
                        z_ref[t * BLK : (t + 1) * BLK, 0:lo] = part
                w_ref[lo:nxt, lo:nxt] = wk
                for t, part in enumerate([wh, wm, wh, wl, wm, wh]):
                    z_ref[t * BLK : (t + 1) * BLK, lo:nxt] = part
                if nxt < size:
                    gh, gm, gl = split3(g_ref[nxt:, lo:nxt])
                    panel = dot32(
                        jnp.concatenate([gh, gh, gm, gh, gm, gl], axis=1),
                        jnp.concatenate([wh, wm, wh, wl, wm, wh], axis=1),
                        NT,
                    )
                    ph, pm, pw = split3(panel)
                    for t, part in enumerate([ph, ph, pm, ph, pm, pw]):
                        x_ref[nxt:, t * BLK : (t + 1) * BLK] = part
                    for t, part in enumerate([ph, pm, ph, pw, pm, ph]):
                        y_ref[nxt:, t * BLK : (t + 1) * BLK] = part
                    j = nxt
                    while j < size:
                        wide = 2 * BLK if j % (2 * BLK) == 0 else BLK
                        g_ref[j:, j : j + wide] -= dot32(
                            x_ref[j:, 0:depth], y_ref[j : j + wide, 0:depth], NT
                        )
                        j += wide
                    w_ref[nxt:, 0:nxt] -= dot32(x_ref[nxt:, 0:depth], z_ref[0:depth, 0:nxt], NN)

        return carry

    lax.fori_loop(0, blocks, step, 0)


class Group:
    def __init__(self, axis, n):
        self.axis, self.n = axis, n
        self.me = lax.axis_index(axis)

    def peer(self, t):
        return lax.rem(self.me + t, self.n)

    def source(self, t):
        return lax.rem(self.me + self.n - t, self.n)

    def each(self, fn):
        def step(t, carry):
            fn(t)
            return carry

        lax.fori_loop(1, self.n, step, 0)

    def copy(self, src, dst, sems, t):
        return pltpu.make_async_remote_copy(
            src_ref=src,
            dst_ref=dst,
            send_sem=sems.at[0, t - 1],
            recv_sem=sems.at[1, t - 1],
            device_id={self.axis: self.peer(t)},
            device_id_type=MESH,
        )

    def greet(self, barrier):
        self.each(
            lambda t: pl.semaphore_signal(
                barrier, inc=1, device_id={self.axis: self.peer(t)}, device_id_type=MESH
            )
        )

    def scatter_start(self, stage, recv, sems):
        self.each(lambda t: self.copy(stage.at[self.peer(t)], recv.at[t - 1], sems, t).start())

    def scatter_finish(self, stage, recv, sems):
        self.each(lambda t: self.copy(stage.at[self.peer(t)], recv.at[t - 1], sems, t).wait())
        return tree_sum([stage[self.me]] + [recv[t] for t in range(self.n - 1)])

    def scatter_sum(self, stage, recv, sems):
        self.scatter_start(stage, recv, sems)
        return self.scatter_finish(stage, recv, sems)

    def gather_start(self, value, out, sems):
        out[self.me] = value
        self.each(lambda t: self.copy(out.at[self.me], out.at[self.me], sems, t).start())

    def gather_finish(self, out, sems):
        def wait(t):
            src = self.source(t)
            self.copy(out.at[src], out.at[src], sems, t).wait_recv()
            self.copy(out.at[self.me], out.at[self.me], sems, t).wait_send()

        self.each(wait)

    def gather(self, value, out, sems):
        self.gather_start(value, out, sems)
        self.gather_finish(out, sems)


CORES = 2
SUBS = 2
DIST = (4, 3, -3, 2, -2, 1, -1, 0)
PLUS = (0, 1, 3, 5)
MINUS = (0, 2, 4, 6)
GOT_PLUS = (1, 3, 5, 7)
GOT_MINUS = (2, 4, 6, 7)


class Line:
    def __init__(self, n_dp):
        self.zs = n_dp // CORES
        me = lax.axis_index("dp")
        self.z = me // CORES
        self.c = lax.rem(me, CORES)

    def to(self, hop):
        chip = lax.rem(self.z + hop + self.zs, self.zs)
        return {"dp": chip * CORES + self.c}

    def partner(self):
        return {"dp": self.z * CORES + (1 - self.c)}

    def copy(self, src, dst, sems, at, device):
        return pltpu.make_async_remote_copy(
            src_ref=src,
            dst_ref=dst,
            send_sem=sems.at[(0, *at)],
            recv_sem=sems.at[(1, *at)],
            device_id=device,
            device_id_type=MESH,
        )


def halves_sent(way, s, first):
    if s == (0 if first else 3):
        return (way,)
    return (0, 1)


def sketch_gram(line, ready, meanwhile, a_ref, s_ref, g_ref, p, pair, ring, gat, gpar, pair_sems, ring_sems, gat_sems, gpar_sems):
    half = p.shape[3]
    sub = half // SUBS
    chunk = 2 * CORES * half
    cols = a_ref.shape[1]
    wide = 2 * LANES

    def partial(*chunks):
        rows = [
            s_ref[
                pl.ds(
                    pl.multiple_of(lax.rem(line.z + DIST[e] + line.zs, line.zs) * chunk, 16), chunk
                ),
                :,
            ]
            for e in chunks
        ]
        left = jnp.concatenate(rows, axis=0)

        def tile(i, carry):
            at = pl.multiple_of(i * wide, wide)
            prod = dot32(left, a_ref[:, pl.ds(at, wide)], NN)
            for n, e in enumerate(chunks):
                for d in range(2):
                    for c in range(CORES):
                        r = n * chunk + (d * CORES + c) * half
                        p[e, d, c, :, pl.ds(at, wide)] = prod[r : r + half]
            return carry

        lax.fori_loop(0, cols // wide, tile, 0)

    def pair_copy(e, d):
        return line.copy(
            p.at[e, d, 1 - line.c], pair.at[e, d], pair_sems, (e, d), line.partner()
        )

    def pair_send(*chunks):
        for e in chunks:
            for d in range(2):
                pair_copy(e, d).start()

    def piece(ref, q):
        return ref.at[pl.ds(q * sub, sub), :]

    def ring_copy(way, s, d, q):
        e = (PLUS, MINUS)[way][s]
        return line.copy(
            piece(p.at[e, d, line.c], q),
            piece(ring.at[way, s, d], q),
            ring_sems,
            (way, s, d, q),
            line.to((1, -1)[way]),
        )

    def ring_step(s):
        for e in sorted({PLUS[s], MINUS[s]}):
            for d in range(2):
                pair_copy(e, d).wait_recv()
        for q in range(SUBS):
            for d in range(2):
                for way in range(2):
                    if d not in halves_sent(way, s, True):
                        continue
                    e = (PLUS, MINUS)[way][s]
                    at = pl.ds(q * sub, sub)
                    value = p[e, d, line.c, at, :] + pair[e, d, at, :]
                    if s > 0 and d in halves_sent(way, s - 1, True):
                        ring_copy(way, s - 1, d, q).wait_recv()
                        value = value + ring[way, s - 1, d, at, :]
                    p[e, d, line.c, at, :] = value
                    ring_copy(way, s, d, q).start()

    def gat_copy(way, s, d, q):
        src = (PLUS, MINUS)[way][s]
        dst = (GOT_PLUS, GOT_MINUS)[way][s]
        return line.copy(
            piece(gat.at[src, d], q),
            piece(gat.at[dst, d], q),
            gat_sems,
            (way, s, d, q),
            line.to((1, -1)[way]),
        )

    def gpar_copy(e, d):
        return line.copy(gat.at[e, d], gpar.at[e, d], gpar_sems, (e, d), line.partner())

    def gather_step(s):
        for q in range(SUBS):
            for d in range(2):
                for way in range(2):
                    if d not in halves_sent(way, s, False):
                        continue
                    gat_copy(way, s, d, q).wait_recv()
                    if s < 3 and d in halves_sent(way, s + 1, False):
                        gat_copy(way, s + 1, d, q).start()
                    if q == SUBS - 1:
                        gpar_copy((GOT_PLUS, GOT_MINUS)[way][s], d).start()

    partial(0)
    ready()
    pair_send(0)
    partial(1, 2)
    pair_send(1, 2)
    ring_step(0)
    partial(3, 4)
    pair_send(3, 4)
    ring_step(1)
    partial(5, 6)
    pair_send(5, 6)
    ring_step(2)
    partial(7)
    pair_send(7)
    g_ref[...] = jnp.zeros_like(g_ref)
    ring_step(3)
    meanwhile()
    for d in range(2):
        pair_copy(7, d).wait_recv()
    for q in range(SUBS):
        for d in range(2):
            at = pl.ds(q * sub, sub)
            value = p[7, d, line.c, at, :] + pair[7, d, at, :]
            for way in range(2):
                ring_copy(way, 3, d, q).wait_recv()
                value = value + ring[way, 3, d, at, :]
            gat[0, d, at, :] = value
            for way in range(2):
                gat_copy(way, 0, d, q).start()
            if q == SUBS - 1:
                gpar_copy(0, d).start()

    def add(e, carry):
        for step, at in ((0, 1), (1, 1), (2, 3), (3, 5)):

            @pl.when(e == at)
            def _():
                gather_step(step)

        for d in range(2):
            gpar_copy(e, d).wait_recv()
        rows = jnp.concatenate([gat[e, 0], gat[e, 1], gpar[e, 0], gpar[e, 1]], axis=0)
        rh, rm, rl = split3(rows)
        th, tm, tl = split3(rows.T)
        for j in range(0, cols, wide):
            high, mid, low = rh[:, j : j + wide], rm[:, j : j + wide], rl[:, j : j + wide]
            g_ref[j:, j : j + wide] += (
                dot32(th[j:], high, NN)
                + (dot32(th[j:], mid, NN) + dot32(tm[j:], high, NN))
                + (dot32(tm[j:], mid, NN) + dot32(th[j:], low, NN) + dot32(tl[j:], high, NN))
            )
        return carry

    lax.fori_loop(0, 8, add, 0)
    for e in range(8):
        for d in range(2):
            pair_copy(e, d).wait_send()
            gpar_copy(e, d).wait_send()
    for s in range(4):
        for way in range(2):
            for q in range(SUBS):
                for d in halves_sent(way, s, True):
                    ring_copy(way, s, d, q).wait_send()
                for d in halves_sent(way, s, False):
                    gat_copy(way, s, d, q).wait_send()


def lane_partial(x):
    return tree_sum(
        [x[:, i : i + LANES] * x[:, i : i + LANES] for i in range(0, x.shape[1], LANES)]
    )


def norm_of(lanes):
    return jnp.sqrt(jnp.sum(lanes, axis=1, keepdims=True) + NORM_EPS)


def put_slices(stage, value, extra):
    n, _, wide = stage.shape
    halves = n * SUB // value.shape[0]
    part = value.shape[1] // halves
    for d in range(n):
        r, h = SUB * (d // halves), part * (d % halves)
        stage[d, :, 0:part] = value[r : r + SUB, h : h + part]
        if extra is not None:
            stage[d, :, part:wide] = extra[r : r + SUB, :]


def take_slices(out, k, part):
    n = out.shape[0]
    halves = n * SUB // k
    value = jnp.concatenate(
        [
            jnp.concatenate([out[g * halves + h, :, 0:part] for h in range(halves)], axis=1)
            for g in range(n // halves)
        ],
        axis=0,
    )
    extra = jnp.concatenate(
        [out[g * halves, :, part : part + LANES] for g in range(n // halves)], axis=0
    )
    return value, extra


def times_exact(x, mat, dims):
    k = x.shape[0]
    both = dot32(jnp.concatenate(split3(x), axis=0), mat, dims)
    return both[0:k] + (both[k : 2 * k] + both[2 * k : 3 * k])


def times_split(x, parts, dims):
    k = x.shape[0]
    high, mid, low = split3(x)
    mh, mm, ml = parts
    a = dot32(jnp.concatenate([high, mid, low], axis=0), mh, dims)
    b = dot32(jnp.concatenate([high, mid], axis=0), mm, dims)
    c = dot32(high, ml, dims)
    return a[0:k] + ((a[k : 2 * k] + b[0:k]) + ((a[2 * k : 3 * k] + b[k : 2 * k]) + c))


def whole_kernel(
    n_dp,
    n_feat,
    a_ref,
    s_ref,
    t_ref,
    sol_ref,
    ratio_ref,
    p,
    pair,
    ring,
    gat,
    gpar,
    pair_sems,
    ring_sems,
    gat_sems,
    gpar_sems,
    g_ref,
    w_ref,
    d_ref,
    wk_ref,
    wh,
    wm,
    wl,
    u_ref,
    img_ref,
    d_stage,
    d_recv,
    d_out,
    d_stage2,
    d_recv2,
    d_out2,
    f_stage,
    f_recv,
    f_out,
    f_stage2,
    f_recv2,
    small_dp,
    small_feat,
    dp_sems,
    feat_sems,
):
    dp = Group("dp", n_dp)
    feat = Group("feat", n_feat)
    k, rows = t_ref.shape
    cols = a_ref.shape[1]
    f_halves = n_feat * SUB // k
    f_part = rows // f_halves
    d_part = cols // (n_dp * SUB // k)

    barrier = pltpu.get_barrier_semaphore()
    dp.greet(barrier)
    feat.greet(barrier)
    def preconditioned(vec):
        return times_split(vec, (wh[...], wm[...], wl[...]), NN)

    def adjoint_pre(vec):
        return times_split(vec, (wh[...], wm[...], wl[...]), NT)

    targets = t_ref[...]

    def ready():
        pl.semaphore_wait(barrier, n_dp + n_feat - 2)

    def meanwhile():
        put_slices(d_stage, times_exact(t_ref[...], a_ref[...], NN), lane_partial(t_ref[...]))

    sketch_gram(
        Line(n_dp), ready, meanwhile, a_ref, s_ref, g_ref, p, pair, ring, gat, gpar,
        pair_sems, ring_sems, gat_sems, gpar_sems,
    )
    dp.scatter_start(d_stage, d_recv, dp_sems.at[0])

    def between():
        total = dp.scatter_finish(d_stage, d_recv, dp_sems.at[0])
        dp.gather_start(total, d_out, dp_sems.at[1])

    factor(g_ref, w_ref, d_ref, wk_ref, wh, wm, wl, between)
    dp.gather_finish(d_out, dp_sems.at[1])
    h, m, l = split3(w_ref[...])
    wh[...] = h
    wm[...] = m
    wl[...] = l
    adj, squares = take_slices(d_out, k, d_part)
    beta_first = norm_of(squares)
    u_ref[...] = targets / beta_first

    v_raw = adjoint_pre(adj / beta_first)
    y_raw = preconditioned(v_raw)
    put_slices(f_stage, times_exact(y_raw, a_ref[...], NT), lane_partial(v_raw))
    total = feat.scatter_sum(f_stage, f_recv, feat_sems.at[0])
    feat.gather(total, f_out, feat_sems.at[1])
    image, squares = take_slices(f_out, k, f_part)
    alpha = norm_of(squares)
    v = v_raw / alpha
    w = y_raw / alpha
    rho_bar = alpha
    phi_bar = beta_first

    u_raw = image / alpha - alpha * u_ref[...]
    put_slices(d_stage2, times_exact(u_raw, a_ref[...], NN), lane_partial(u_raw))
    total = dp.scatter_sum(d_stage2, d_recv2, dp_sems.at[2])
    dp.gather(total, d_out2, dp_sems.at[3])
    adj, squares = take_slices(d_out2, k, d_part)
    beta = norm_of(squares)
    u_ref[...] = u_raw / beta
    rho = jnp.sqrt(rho_bar * rho_bar + beta * beta)
    cosine = rho_bar / rho
    sine = beta / rho
    phi = cosine * phi_bar
    phi_bar = sine * phi_bar
    coords = (phi / rho) * w
    v_raw = adjoint_pre(adj / beta) - beta * v
    y_raw = preconditioned(v_raw)

    put_slices(f_stage2, times_exact(y_raw, a_ref[...], NT), lane_partial(v_raw))
    put_slices(img_ref, u_ref[...], None)
    total = feat.scatter_sum(f_stage2, f_recv2, feat_sems.at[2])
    squares = total[:, f_part:]
    alpha = norm_of(squares)
    left = total[:, 0:f_part] / alpha - alpha * img_ref[feat.me]
    dp.gather(lane_partial(left), small_dp, dp_sems.at[4])
    norms = tree_sum([small_dp[i] for i in range(n_dp)])
    feat.gather(jnp.concatenate([norms, squares], axis=1), small_feat, feat_sems.at[3])
    groups = n_feat // f_halves
    norms = jnp.concatenate(
        [
            tree_sum([small_feat[g * f_halves + i, :, 0:LANES] for i in range(f_halves)])
            for g in range(groups)
        ],
        axis=0,
    )
    squares = jnp.concatenate([small_feat[g * f_halves, :, LANES:] for g in range(groups)], axis=0)
    alpha = norm_of(squares)
    theta = sine * alpha
    rho_bar = -cosine * alpha
    w = y_raw / alpha - (theta / rho) * w
    beta = norm_of(norms)
    rho = jnp.sqrt(rho_bar * rho_bar + beta * beta)
    cosine = rho_bar / rho
    sine = beta / rho
    phi = cosine * phi_bar
    phi_bar = sine * phi_bar
    sol_ref[...] = coords + (phi / rho) * w
    ratio_ref[...] = jnp.broadcast_to(phi_bar / beta_first, ratio_ref.shape)


def whole(design, sketch, targets, n_dp, n_feat):
    rows, cols = design.shape
    k = targets.shape[0]
    zs = n_dp // CORES
    half = sketch.shape[0] // (2 * n_dp)
    d_wide = cols * k // (n_dp * SUB) + LANES
    f_wide = rows * k // (n_feat * SUB) + LANES
    vmem = pl.BlockSpec(memory_space=pltpu.VMEM)
    sems = pltpu.SemaphoreType.DMA
    d_bufs = [
        pltpu.VMEM((n_dp, SUB, d_wide), F32),
        pltpu.VMEM((n_dp - 1, SUB, d_wide), F32),
        pltpu.VMEM((n_dp, SUB, d_wide), F32),
    ]
    f_bufs = [
        pltpu.VMEM((n_feat, SUB, f_wide), F32),
        pltpu.VMEM((n_feat - 1, SUB, f_wide), F32),
        pltpu.VMEM((n_feat, SUB, f_wide), F32),
    ]
    return pl.pallas_call(
        functools.partial(whole_kernel, n_dp, n_feat),
        out_shape=(
            jax.ShapeDtypeStruct((k, cols), F32),
            jax.ShapeDtypeStruct((k, LANES), F32),
        ),
        in_specs=[vmem] * 3,
        out_specs=(vmem, vmem),
        scratch_shapes=[
            pltpu.VMEM((zs, 2, CORES, half, cols), F32),
            pltpu.VMEM((zs, 2, half, cols), F32),
            pltpu.VMEM((2, 4, 2, half, cols), F32),
            pltpu.VMEM((zs, 2, half, cols), F32),
            pltpu.VMEM((zs, 2, half, cols), F32),
            sems((2, zs, 2)),
            sems((2, 2, 4, 2, SUBS)),
            sems((2, 2, 4, 2, SUBS)),
            sems((2, zs, 2)),
            pltpu.VMEM((cols, cols), F32),
            pltpu.VMEM((cols, cols), F32),
            pltpu.VMEM((BLK, BLK), F32),
            pltpu.VMEM((BLK, BLK), F32),
        ]
        + [pltpu.VMEM((cols, cols), BF16)] * 3
        + [
            pltpu.VMEM((k, rows), F32),
            pltpu.VMEM((n_feat, SUB, f_wide - LANES), F32),
        ]
        + d_bufs
        + d_bufs
        + f_bufs
        + f_bufs[:2]
        + [
            pltpu.VMEM((n_dp, SUB, LANES), F32),
            pltpu.VMEM((n_feat, SUB, 2 * LANES), F32),
            sems((5, 2, n_dp - 1)),
            sems((4, 2, n_feat - 1)),
        ],
        compiler_params=pltpu.CompilerParams(
            collective_id=0, has_side_effects=True, vmem_limit_bytes=62 * MIB
        ),
    )(design, sketch, targets)


def body(n_dp, n_feat, design, sketch, targets):
    sol, ratio = whole(design, sketch, targets, n_dp, n_feat)
    return sol, ratio[:, 0]


def solution(mesh):
    return jax.shard_map(
        functools.partial(body, mesh.shape["dp"], mesh.shape["feat"]),
        mesh=mesh,
        in_specs=(P("dp", "feat"), P(None, "dp"), P(None, "dp")),
        out_specs=(P(None, "feat"), P()),
        check_vma=False,
    )
```

```python
import functools

import jax
import jax.numpy as jnp
from jax import lax
from jax.experimental import pallas as pl
from jax.experimental.pallas import tpu as pltpu
from jax.sharding import PartitionSpec as P

NORM_EPS = 1e-06
F32 = jnp.float32
BF16 = jnp.bfloat16
MESH = pl.DeviceIdType.MESH
NN = ((1,), (0,))
NT = ((1,), (1,))
SUB = 8
LANES = 128
BLK = 128
MIB = 2**20
PARTS = 2


def split3(x):
    high = x.astype(BF16)
    rest = x - high.astype(F32)
    mid = rest.astype(BF16)
    return high, mid, (rest - mid.astype(F32)).astype(BF16)


def dot32(a, b, dims):
    return lax.dot_general(a, b, (dims, ((), ())), preferred_element_type=F32)


def lane_splat(x, c):
    return jnp.broadcast_to(x[:, c : c + 1], x.shape)


def row_splat(x, r):
    return jnp.broadcast_to(x[r : r + 1, :], x.shape)


def tree_sum(terms):
    while len(terms) > 1:
        terms = [
            terms[i] + terms[i + 1] if i + 1 < len(terms) else terms[i]
            for i in range(0, len(terms), 2)
        ]
    return terms[0]


def factor_block(d_ref, w_ref):
    tiles = BLK // SUB
    pivots = 2 * SUB
    rid = lax.broadcasted_iota(jnp.int32, (SUB, BLK), 0)
    lid = lax.broadcasted_iota(jnp.int32, (SUB, BLK), 1)
    a = [d_ref[SUB * i : SUB * i + SUB, :] for i in range(tiles)]
    w = [jnp.where(lid == rid + SUB * i, 1.0, 0.0) for i in range(tiles)]
    for first in range(0, tiles, 2):
        lane = SUB * first
        cols = [[lane_splat(a[first + t], lane + c) for t in range(2)] for c in range(pivots)]
        rows_a = [a[first], a[first + 1]]
        rows_w = [w[first], w[first + 1]]
        low_w = [w[first], w[first + 1]]
        inv_pivots = [jnp.zeros((SUB, BLK), F32) for _ in range(2)]
        pivot = row_splat(cols[0][0], 0)
        for k in range(pivots):
            h, r = divmod(k, SUB)
            inv = 1.0 / pivot
            if k + 1 < pivots:
                h1, r1 = divmod(k + 1, SUB)
                off = row_splat(cols[k + 1][h], r)
                pivot = row_splat(cols[k + 1][h1], r1) - (off * off) * inv
            mult = [
                (jnp.where(rid == r, 0.0, cols[k][t]) if t == h else cols[k][t]) * inv
                for t in range(2)
            ]
            below = [jnp.where(rid > r, mult[t], 0.0) if t == h else mult[t] for t in range(2)]
            for j in range(k + 1, pivots):
                line = row_splat(cols[j][h], r)
                cols[j] = [cols[j][t] - mult[t] * line for t in range(2)]
            line_a, line_w, line_l = (row_splat(x[h], r) for x in (rows_a, rows_w, low_w))
            rows_a = [rows_a[t] - mult[t] * line_a for t in range(2)]
            rows_w = [rows_w[t] - mult[t] * line_w for t in range(2)]
            low_w = [low_w[t] - below[t] * line_l if t >= h else low_w[t] for t in range(2)]
            inv_pivots[h] = jnp.where(rid == r, inv, inv_pivots[h])
        for t in range(2):
            rows_a[t] = rows_a[t] * inv_pivots[t]
            rows_w[t] = rows_w[t] * inv_pivots[t]
            at = lane + SUB * t
            w_ref[at : at + SUB, :] = low_w[t] * jnp.sqrt(inv_pivots[t])
        if first + 2 < tiles:
            splat_a = [row_splat(rows_a[c // SUB], c % SUB) for c in range(pivots)]
            splat_w = [row_splat(rows_w[c // SUB], c % SUB) for c in range(pivots)]
            for i in range(first + 2, tiles):
                p = [lane_splat(a[i], lane + c) for c in range(pivots)]
                a[i] = a[i] - tree_sum([p[c] * splat_a[c] for c in range(pivots)])
                w[i] = w[i] - tree_sum([p[c] * splat_w[c] for c in range(pivots)])


def factor(g_ref, w_ref, d_ref, wk_ref, x_ref, y_ref, z_ref, between):
    size = g_ref.shape[0]
    blocks = size // BLK
    depth = 6 * BLK
    w_ref[...] = jnp.zeros_like(w_ref)

    def step(k, carry):
        at = pl.multiple_of(k * BLK, BLK)
        d_ref[...] = g_ref[pl.ds(at, BLK), pl.ds(at, BLK)]
        factor_block(d_ref, wk_ref)
        for this in range(blocks):

            @pl.when(k == this)
            def _():
                if this == 2:
                    between()
                lo = this * BLK
                nxt = lo + BLK
                wk = wk_ref[...]
                wh, wm, wl = split3(wk)
                if this > 0:
                    ah, am, al = split3(w_ref[lo:nxt, 0:lo])
                    row = dot32(
                        jnp.concatenate([wh, wh, wm, wh, wm, wl], axis=1),
                        jnp.concatenate([ah, am, ah, al, am, ah], axis=0),
                        NN,
                    )
                    w_ref[lo:nxt, 0:lo] = row
                    rh, rm, rl = split3(row)
                    for t, part in enumerate([rh, rm, rh, rl, rm, rh]):
                        z_ref[t * BLK : (t + 1) * BLK, 0:lo] = part
                w_ref[lo:nxt, lo:nxt] = wk
                for t, part in enumerate([wh, wm, wh, wl, wm, wh]):
                    z_ref[t * BLK : (t + 1) * BLK, lo:nxt] = part
                if nxt < size:
                    gh, gm, gl = split3(g_ref[nxt:, lo:nxt])
                    panel = dot32(
                        jnp.concatenate([gh, gh, gm, gh, gm, gl], axis=1),
                        jnp.concatenate([wh, wm, wh, wl, wm, wh], axis=1),
                        NT,
                    )
                    ph, pm, pw = split3(panel)
                    for t, part in enumerate([ph, ph, pm, ph, pm, pw]):
                        x_ref[nxt:, t * BLK : (t + 1) * BLK] = part
                    for t, part in enumerate([ph, pm, ph, pw, pm, ph]):
                        y_ref[nxt:, t * BLK : (t + 1) * BLK] = part
                    j = nxt
                    while j < size:
                        wide = 2 * BLK if j % (2 * BLK) == 0 else BLK
                        g_ref[j:, j : j + wide] -= dot32(
                            x_ref[j:, 0:depth], y_ref[j : j + wide, 0:depth], NT
                        )
                        j += wide
                    w_ref[nxt:, 0:nxt] -= dot32(x_ref[nxt:, 0:depth], z_ref[0:depth, 0:nxt], NN)

        return carry

    lax.fori_loop(0, blocks, step, 0)


class Group:
    def __init__(self, axis, n):
        self.axis, self.n = axis, n
        self.me = lax.axis_index(axis)
        self.unsent = []

    def peer(self, t):
        return lax.rem(self.me + t, self.n)

    def source(self, t):
        return lax.rem(self.me + self.n - t, self.n)

    def each(self, fn):
        def step(t, carry):
            fn(t)
            return carry

        lax.fori_loop(1, self.n, step, 0)

    def copy(self, src, dst, sems, t):
        return pltpu.make_async_remote_copy(
            src_ref=src,
            dst_ref=dst,
            send_sem=sems.at[0, t - 1],
            recv_sem=sems.at[1, t - 1],
            device_id={self.axis: self.peer(t)},
            device_id_type=MESH,
        )

    def greet(self, barrier):
        self.each(
            lambda t: pl.semaphore_signal(
                barrier, inc=1, device_id={self.axis: self.peer(t)}, device_id_type=MESH
            )
        )

    def scatter_start(self, stage, recv, sems):
        self.each(lambda t: self.copy(stage.at[self.peer(t)], recv.at[t - 1], sems, t).start())

    def scatter_finish(self, stage, recv, sems, later=True):
        self.each(lambda t: self.copy(stage.at[self.peer(t)], recv.at[t - 1], sems, t).wait_recv())

        def copy(t):
            return self.copy(stage.at[self.peer(t)], recv.at[t - 1], sems, t)

        if later:
            self.unsent.append(copy)
        else:
            self.each(lambda t: copy(t).wait_send())
        return tree_sum([stage[self.me]] + [recv[t] for t in range(self.n - 1)])

    def scatter_sum(self, stage, recv, sems):
        self.scatter_start(stage, recv, sems)
        return self.scatter_finish(stage, recv, sems)

    def gather_start(self, value, out, sems):
        out[self.me] = value
        self.each(lambda t: self.copy(out.at[self.me], out.at[self.me], sems, t).start())

    def gather_finish(self, out, sems):
        def wait(t):
            src = self.source(t)
            self.copy(out.at[src], out.at[src], sems, t).wait_recv()

        self.each(wait)
        self.unsent.append(lambda t: self.copy(out.at[self.me], out.at[self.me], sems, t))

    def finish_sends(self):
        for copy in self.unsent:
            self.each(lambda t: copy(t).wait_send())

    def gather(self, value, out, sems):
        self.gather_start(value, out, sems)
        self.gather_finish(out, sems)


CORES = 2
SUBS = 2
DIST = (4, 3, -3, 2, -2, 1, -1, 0)
PLUS = (0, 1, 3, 5)
MINUS = (0, 2, 4, 6)
GOT_PLUS = (1, 3, 5, 7)
GOT_MINUS = (2, 4, 6, 7)


class Line:
    def __init__(self, n_dp):
        self.zs = n_dp // CORES
        me = lax.axis_index("dp")
        self.z = me // CORES
        self.c = lax.rem(me, CORES)

    def to(self, hop):
        chip = lax.rem(self.z + hop + self.zs, self.zs)
        return {"dp": chip * CORES + self.c}

    def partner(self):
        return {"dp": self.z * CORES + (1 - self.c)}

    def copy(self, src, dst, sems, at, device):
        return pltpu.make_async_remote_copy(
            src_ref=src,
            dst_ref=dst,
            send_sem=sems.at[(0, *at)],
            recv_sem=sems.at[(1, *at)],
            device_id=device,
            device_id_type=MESH,
        )


def halves_sent(way, s, first):
    if s == (0 if first else 3):
        return (way,)
    return (0, 1)


def sketch_gram(line, ready, loaded, meanwhile, a_ref, s_ref, g_ref, p, pair, ring, gat, gpar, pair_sems, ring_sems, gat_sems, gpar_sems):
    half = p.shape[3]
    sub = half // SUBS
    chunk = 2 * CORES * half
    cols = a_ref.shape[1]
    wide = 2 * LANES

    def partial(*chunks):
        for e in chunks:
            loaded(e)
        rows = [
            s_ref[
                pl.ds(
                    pl.multiple_of(lax.rem(line.z + DIST[e] + line.zs, line.zs) * chunk, 16), chunk
                ),
                :,
            ]
            for e in chunks
        ]
        left = jnp.concatenate(rows, axis=0)

        def tile(i, carry):
            at = pl.multiple_of(i * wide, wide)
            prod = dot32(left, a_ref[:, pl.ds(at, wide)], NN)
            for n, e in enumerate(chunks):
                for d in range(2):
                    for c in range(CORES):
                        r = n * chunk + (d * CORES + c) * half
                        p[e, d, c, :, pl.ds(at, wide)] = prod[r : r + half]
            return carry

        lax.fori_loop(0, cols // wide, tile, 0)

    def pair_copy(e, d):
        return line.copy(
            p.at[e, d, 1 - line.c], pair.at[e, d], pair_sems, (e, d), line.partner()
        )

    def pair_send(*chunks):
        for e in chunks:
            for d in range(2):
                pair_copy(e, d).start()

    def piece(ref, q):
        return ref.at[pl.ds(q * sub, sub), :]

    def ring_copy(way, s, d, q):
        e = (PLUS, MINUS)[way][s]
        return line.copy(
            piece(p.at[e, d, line.c], q),
            piece(ring.at[way, s, d], q),
            ring_sems,
            (way, s, d, q),
            line.to((1, -1)[way]),
        )

    def ring_step(s):
        for e in sorted({PLUS[s], MINUS[s]}):
            for d in range(2):
                pair_copy(e, d).wait_recv()
        for q in range(SUBS):
            for turn in range(2):
                for way in range(2):
                    d = (1 - turn, turn)[way]
                    if d not in halves_sent(way, s, True):
                        continue
                    e = (PLUS, MINUS)[way][s]
                    at = pl.ds(q * sub, sub)
                    value = p[e, d, line.c, at, :] + pair[e, d, at, :]
                    if s > 0 and d in halves_sent(way, s - 1, True):
                        ring_copy(way, s - 1, d, q).wait_recv()
                        value = value + ring[way, s - 1, d, at, :]
                    p[e, d, line.c, at, :] = value
                    ring_copy(way, s, d, q).start()

    def gat_copy(way, s, d, q):
        src = (PLUS, MINUS)[way][s]
        dst = (GOT_PLUS, GOT_MINUS)[way][s]
        return line.copy(
            piece(gat.at[src, d], q),
            piece(gat.at[dst, d], q),
            gat_sems,
            (way, s, d, q),
            line.to((1, -1)[way]),
        )

    def gpar_copy(e, d):
        return line.copy(gat.at[e, d], gpar.at[e, d], gpar_sems, (e, d), line.partner())

    def gather_step(s):
        for q in range(SUBS):
            for d in range(2):
                for way in range(2):
                    if d not in halves_sent(way, s, False):
                        continue
                    gat_copy(way, s, d, q).wait_recv()
                    if s < 3 and d in halves_sent(way, s + 1, False):
                        gat_copy(way, s + 1, d, q).start()
                    if q == SUBS - 1:
                        gpar_copy((GOT_PLUS, GOT_MINUS)[way][s], d).start()

    partial(0)
    ready()
    pair_send(0)
    ring_step(0)
    partial(1, 2)
    pair_send(1, 2)
    ring_step(1)
    partial(3, 4)
    pair_send(3, 4)
    partial(5, 6)
    pair_send(5, 6)
    ring_step(2)
    partial(7)
    pair_send(7)
    g_ref[...] = jnp.zeros_like(g_ref)
    ring_step(3)
    meanwhile()
    for d in range(2):
        pair_copy(7, d).wait_recv()
    for q in range(SUBS):
        for d in range(2):
            at = pl.ds(q * sub, sub)
            value = p[7, d, line.c, at, :] + pair[7, d, at, :]
            for way in range(2):
                ring_copy(way, 3, d, q).wait_recv()
                value = value + ring[way, 3, d, at, :]
            gat[0, d, at, :] = value
            for way in range(2):
                gat_copy(way, 0, d, q).start()
            if q == SUBS - 1:
                gpar_copy(0, d).start()

    def add(e, carry):
        for step, at in ((0, 1), (1, 1), (2, 3), (3, 7)):

            @pl.when(e == at)
            def _():
                gather_step(step)

        for d in range(2):
            gpar_copy(e, d).wait_recv()
        rows = jnp.concatenate([gat[e, 0], gat[e, 1], gpar[e, 0], gpar[e, 1]], axis=0)
        rh, rm, rl = split3(rows)
        th, tm, tl = split3(rows.T)
        for j in range(0, cols, wide):
            high, mid, low = rh[:, j : j + wide], rm[:, j : j + wide], rl[:, j : j + wide]
            g_ref[j:, j : j + wide] += (
                dot32(th[j:], high, NN)
                + (dot32(th[j:], mid, NN) + dot32(tm[j:], high, NN))
                + (dot32(tm[j:], mid, NN) + dot32(th[j:], low, NN) + dot32(tl[j:], high, NN))
            )
        return carry

    lax.fori_loop(0, 8, add, 0)
    for e in range(8):
        for d in range(2):
            pair_copy(e, d).wait_send()
            gpar_copy(e, d).wait_send()
    for s in range(4):
        for way in range(2):
            for q in range(SUBS):
                for d in halves_sent(way, s, True):
                    ring_copy(way, s, d, q).wait_send()
                for d in halves_sent(way, s, False):
                    gat_copy(way, s, d, q).wait_send()


class Chips(Group):
    def __init__(self, line):
        self.axis, self.n, self.me, self.c = "dp", line.zs, line.z, line.c
        self.unsent = []

    def copy(self, src, dst, sems, t):
        return pltpu.make_async_remote_copy(
            src_ref=src,
            dst_ref=dst,
            send_sem=sems.at[0, t - 1],
            recv_sem=sems.at[1, t - 1],
            device_id={"dp": self.peer(t) * CORES + self.c},
            device_id_type=MESH,
        )


def pair_and_chips_sum(line, value, extra, halves, got, stage, recv, out, sems, pair_sems):
    chips = Chips(line)
    part = value.shape[1] // CORES
    for h in range(CORES):
        halves[h, :, 0:part] = value[:, h * part : (h + 1) * part]
        halves[h, :, part:] = extra
    to_other = line.copy(halves.at[1 - line.c], got, pair_sems, (0,), line.partner())
    to_other.start()
    to_other.wait_recv()
    both = halves[line.c] + got[...]
    for d in range(chips.n):
        stage[d] = both[SUB * d : SUB * d + SUB]
    total = chips.scatter_sum(stage, recv, sems.at[0])
    chips.gather(total, out.at[line.c], sems.at[1])
    back = line.copy(out.at[line.c], out.at[line.c], pair_sems, (1,), line.partner())
    back.start()
    back.wait()
    to_other.wait_send()
    chips.finish_sends()
    rows = value.shape[0]
    total = jnp.concatenate(
        [out[h].reshape(rows, part + LANES)[:, 0:part] for h in range(CORES)], axis=1
    )
    return total, out[0].reshape(rows, part + LANES)[:, part:]


def lane_partial(x):
    return tree_sum(
        [x[:, i : i + LANES] * x[:, i : i + LANES] for i in range(0, x.shape[1], LANES)]
    )


def norm_of(lanes):
    return jnp.sqrt(jnp.sum(lanes, axis=1, keepdims=True) + NORM_EPS)


def put_slices(stage, value, extra):
    n, _, wide = stage.shape
    halves = n * SUB // value.shape[0]
    part = value.shape[1] // halves
    for d in range(n):
        r, h = SUB * (d // halves), part * (d % halves)
        stage[d, :, 0:part] = value[r : r + SUB, h : h + part]
        if extra is not None:
            stage[d, :, part:wide] = extra[r : r + SUB, :]


def take_slices(out, k, part):
    n = out.shape[0]
    halves = n * SUB // k
    value = jnp.concatenate(
        [
            jnp.concatenate([out[g * halves + h, :, 0:part] for h in range(halves)], axis=1)
            for g in range(n // halves)
        ],
        axis=0,
    )
    return value


def take_extra(out, k, part):
    n = out.shape[0]
    halves = n * SUB // k
    return jnp.concatenate(
        [out[g * halves, :, part : part + LANES] for g in range(n // halves)], axis=0
    )


def times_exact(x, mat, dims):
    k = x.shape[0]
    both = dot32(jnp.concatenate(split3(x), axis=0), mat, dims)
    return both[0:k] + (both[k : 2 * k] + both[2 * k : 3 * k])


def times_split(x, parts, dims):
    k = x.shape[0]
    high, mid, low = split3(x)
    mh, mm, ml = parts
    a = dot32(jnp.concatenate([high, mid, low], axis=0), mh, dims)
    b = dot32(jnp.concatenate([high, mid], axis=0), mm, dims)
    c = dot32(high, ml, dims)
    return a[0:k] + ((a[k : 2 * k] + b[0:k]) + ((a[2 * k : 3 * k] + b[k : 2 * k]) + c))


def whole_kernel(
    n_dp,
    n_feat,
    a_hbm,
    s_hbm,
    t_ref,
    sol_ref,
    ratio_ref,
    a_ref,
    s_ref,
    load_sems,
    p,
    pair,
    ring,
    gat,
    gpar,
    pair_sems,
    ring_sems,
    gat_sems,
    gpar_sems,
    g_ref,
    w_ref,
    d_ref,
    wk_ref,
    wh,
    wm,
    wl,
    u_ref,
    img_ref,
    d_stage,
    d_recv,
    d_out,
    d_halves,
    d_got,
    d_stage2,
    d_recv2,
    d_out2,
    f_stage,
    f_recv,
    f_out,
    f_stage_b,
    f_recv_b,
    f_out_b,
    f_stage2,
    f_recv2,
    f_stage2_b,
    f_recv2_b,
    small_dp,
    small_feat,
    dp_sems,
    feat_sems,
    chip_sems,
    chip_pair_sems,
):
    dp = Group("dp", n_dp)
    feat = Group("feat", n_feat)
    k, rows = t_ref.shape
    cols = a_ref.shape[1]
    f_halves = n_feat * SUB // k
    part_rows = rows // PARTS
    f_part = part_rows // f_halves
    d_part = cols // (n_dp * SUB // k)

    line = Line(n_dp)
    chunk = s_ref.shape[0] // line.zs

    def load(e):
        at = pl.ds(
            pl.multiple_of(lax.rem(line.z + DIST[e] + line.zs, line.zs) * chunk, 16), chunk
        )
        return pltpu.make_async_copy(s_hbm.at[at, :], s_ref.at[at, :], load_sems.at[e])

    design_load = pltpu.make_async_copy(a_hbm, a_ref, load_sems.at[line.zs])
    load(0).start()
    design_load.start()
    for e in range(1, line.zs):
        load(e).start()

    def loaded(e):
        if e == 0:
            design_load.wait()
        load(e).wait()

    barrier = pltpu.get_barrier_semaphore()
    dp.greet(barrier)
    feat.greet(barrier)
    def preconditioned(vec):
        return times_split(vec, (wh[...], wm[...], wl[...]), NN)

    def adjoint_pre(vec):
        return times_split(vec, (wh[...], wm[...], wl[...]), NT)

    targets = t_ref[...]

    def ready():
        pl.semaphore_wait(barrier, n_dp + n_feat - 2)

    def meanwhile():
        put_slices(d_stage, times_exact(t_ref[...], a_ref[...], NN), lane_partial(t_ref[...]))

    sketch_gram(
        line, ready, loaded, meanwhile, a_ref, s_ref, g_ref, p, pair, ring, gat, gpar,
        pair_sems, ring_sems, gat_sems, gpar_sems,
    )
    dp.scatter_start(d_stage, d_recv, dp_sems.at[0])

    def between():
        total = dp.scatter_finish(d_stage, d_recv, dp_sems.at[0], later=False)
        dp.gather_start(total, d_out, dp_sems.at[1])

    factor(g_ref, w_ref, d_ref, wk_ref, wh, wm, wl, between)
    dp.gather_finish(d_out, dp_sems.at[1])
    h, m, l = split3(w_ref[...])
    wh[...] = h
    wm[...] = m
    wl[...] = l
    adj, squares = take_slices(d_out, k, d_part), take_extra(d_out, k, d_part)
    beta_first = norm_of(squares)
    u_ref[...] = targets / beta_first

    v_raw = adjoint_pre(adj / beta_first)
    y_raw = preconditioned(v_raw)
    def image_start(y, v, stages, recvs, sems):
        for i in range(PARTS):
            at = i * part_rows
            image = times_exact(y, a_ref[at : at + part_rows, :], NT)
            put_slices(stages[i], image, lane_partial(v) if i == 0 else None)
            feat.scatter_start(stages[i], recvs[i], feat_sems.at[sems + i])

    image_start(y_raw, v_raw, (f_stage, f_stage_b), (f_recv, f_recv_b), 0)
    for i, (stage, recv, out) in enumerate(
        ((f_stage, f_recv, f_out), (f_stage_b, f_recv_b, f_out_b))
    ):
        total = feat.scatter_finish(stage, recv, feat_sems.at[i])
        feat.gather_start(total, out, feat_sems.at[PARTS + i])
    feat.gather_finish(f_out, feat_sems.at[PARTS])
    squares = take_extra(f_out, k, f_part)
    alpha = norm_of(squares)
    v = v_raw / alpha
    w = y_raw / alpha
    rho_bar = alpha
    phi_bar = beta_first

    adj = jnp.zeros((k, cols), F32)
    squares = jnp.zeros((k, LANES), F32)
    for i, out in enumerate((f_out, f_out_b)):
        at = i * part_rows
        if i:
            feat.gather_finish(out, feat_sems.at[PARTS + i])
        part = take_slices(out, k, f_part) / alpha - alpha * u_ref[:, at : at + part_rows]
        u_ref[:, at : at + part_rows] = part
        adj = adj + times_exact(part, a_ref[at : at + part_rows, :], NN)
        squares = squares + lane_partial(part)
    adj, squares = pair_and_chips_sum(
        line, adj, squares, d_halves, d_got, d_stage2, d_recv2, d_out2, chip_sems, chip_pair_sems
    )
    beta = norm_of(squares)
    u_ref[...] = u_ref[...] / beta
    rho = jnp.sqrt(rho_bar * rho_bar + beta * beta)
    cosine = rho_bar / rho
    sine = beta / rho
    phi = cosine * phi_bar
    phi_bar = sine * phi_bar
    coords = (phi / rho) * w
    v_raw = adjoint_pre(adj / beta) - beta * v
    y_raw = preconditioned(v_raw)

    image_start(y_raw, v_raw, (f_stage2, f_stage2_b), (f_recv2, f_recv2_b), 2 * PARTS)
    for i in range(PARTS):
        put_slices(img_ref.at[i], u_ref[:, i * part_rows : (i + 1) * part_rows], None)
    total = feat.scatter_finish(f_stage2, f_recv2, feat_sems.at[2 * PARTS])
    squares = total[:, f_part:]
    alpha = norm_of(squares)
    left = lane_partial(total[:, 0:f_part] / alpha - alpha * img_ref[0, feat.me])
    total = feat.scatter_finish(f_stage2_b, f_recv2_b, feat_sems.at[2 * PARTS + 1])
    left = left + lane_partial(total / alpha - alpha * img_ref[1, feat.me])
    dp.gather(left, small_dp, dp_sems.at[2])
    norms = tree_sum([small_dp[i] for i in range(n_dp)])
    feat.gather(jnp.concatenate([norms, squares], axis=1), small_feat, feat_sems.at[3 * PARTS])
    groups = n_feat // f_halves
    norms = jnp.concatenate(
        [
            tree_sum([small_feat[g * f_halves + i, :, 0:LANES] for i in range(f_halves)])
            for g in range(groups)
        ],
        axis=0,
    )
    squares = jnp.concatenate([small_feat[g * f_halves, :, LANES:] for g in range(groups)], axis=0)
    alpha = norm_of(squares)
    theta = sine * alpha
    rho_bar = -cosine * alpha
    w = y_raw / alpha - (theta / rho) * w
    beta = norm_of(norms)
    rho = jnp.sqrt(rho_bar * rho_bar + beta * beta)
    cosine = rho_bar / rho
    sine = beta / rho
    phi = cosine * phi_bar
    phi_bar = sine * phi_bar
    sol_ref[...] = coords + (phi / rho) * w
    ratio_ref[...] = jnp.broadcast_to(phi_bar / beta_first, ratio_ref.shape)
    dp.finish_sends()
    feat.finish_sends()


def whole(design, sketch, targets, n_dp, n_feat):
    rows, cols = design.shape
    k = targets.shape[0]
    zs = n_dp // CORES
    half = sketch.shape[0] // (2 * n_dp)
    d_wide = cols * k // (n_dp * SUB) + LANES
    f_part = rows * k // (n_feat * SUB * PARTS)
    vmem = pl.BlockSpec(memory_space=pltpu.VMEM)
    sems = pltpu.SemaphoreType.DMA
    d_bufs = [
        pltpu.VMEM((n_dp, SUB, d_wide), F32),
        pltpu.VMEM((n_dp - 1, SUB, d_wide), F32),
        pltpu.VMEM((n_dp, SUB, d_wide), F32),
    ]
    f_bufs, f_bufs_b = (
        [
            pltpu.VMEM((n_feat, SUB, wide), F32),
            pltpu.VMEM((n_feat - 1, SUB, wide), F32),
            pltpu.VMEM((n_feat, SUB, wide), F32),
        ]
        for wide in (f_part + LANES, f_part)
    )
    return pl.pallas_call(
        functools.partial(whole_kernel, n_dp, n_feat),
        out_shape=(
            jax.ShapeDtypeStruct((k, cols), F32),
            jax.ShapeDtypeStruct((k, LANES), F32),
        ),
        in_specs=[pl.BlockSpec(memory_space=pl.ANY)] * 2 + [vmem],
        out_specs=(vmem, vmem),
        scratch_shapes=[
            pltpu.VMEM(design.shape, BF16),
            pltpu.VMEM(sketch.shape, BF16),
            sems((zs + 1,)),
            pltpu.VMEM((zs, 2, CORES, half, cols), F32),
            pltpu.VMEM((zs, 2, half, cols), F32),
            pltpu.VMEM((2, 4, 2, half, cols), F32),
            pltpu.VMEM((zs, 2, half, cols), F32),
            pltpu.VMEM((zs, 2, half, cols), F32),
            sems((2, zs, 2)),
            sems((2, 2, 4, 2, SUBS)),
            sems((2, 2, 4, 2, SUBS)),
            sems((2, zs, 2)),
            pltpu.VMEM((cols, cols), F32),
            pltpu.VMEM((cols, cols), F32),
            pltpu.VMEM((BLK, BLK), F32),
            pltpu.VMEM((BLK, BLK), F32),
        ]
        + [pltpu.VMEM((cols, cols), BF16)] * 3
        + [
            pltpu.VMEM((k, rows), F32),
            pltpu.VMEM((PARTS, n_feat, SUB, f_part), F32),
        ]
        + d_bufs
        + [
            pltpu.VMEM((CORES, k, cols // CORES + LANES), F32),
            pltpu.VMEM((k, cols // CORES + LANES), F32),
            pltpu.VMEM((zs, SUB, cols // CORES + LANES), F32),
            pltpu.VMEM((zs - 1, SUB, cols // CORES + LANES), F32),
            pltpu.VMEM((CORES, zs, SUB, cols // CORES + LANES), F32),
        ]
        + f_bufs
        + f_bufs_b
        + f_bufs[:2]
        + f_bufs_b[:2]
        + [
            pltpu.VMEM((n_dp, SUB, LANES), F32),
            pltpu.VMEM((n_feat, SUB, 2 * LANES), F32),
            sems((3, 2, n_dp - 1)),
            sems((3 * PARTS + 1, 2, n_feat - 1)),
            sems((2, 2, zs - 1)),
            sems((2, 2)),
        ],
        compiler_params=pltpu.CompilerParams(
            collective_id=0, has_side_effects=True, vmem_limit_bytes=62 * MIB
        ),
    )(design, sketch, targets)


def body(n_dp, n_feat, design, sketch, targets):
    sol, ratio = whole(design, sketch, targets, n_dp, n_feat)
    return sol, ratio[:, 0]


def solution(mesh):
    return jax.shard_map(
        functools.partial(body, mesh.shape["dp"], mesh.shape["feat"]),
        mesh=mesh,
        in_specs=(P("dp", "feat"), P(None, "dp"), P(None, "dp")),
        out_specs=(P(None, "feat"), P()),
        check_vma=False,
    )
```

```python
import functools

import jax
import jax.numpy as jnp
from jax import lax
from jax.experimental import pallas as pl
from jax.experimental.pallas import tpu as pltpu
from jax.sharding import PartitionSpec as P

NORM_EPS = 1e-06
F32 = jnp.float32
BF16 = jnp.bfloat16
MESH = pl.DeviceIdType.MESH
NN = ((1,), (0,))
NT = ((1,), (1,))
SUB = 8
LANES = 128
BLK = 128
MIB = 2**20
PARTS = 2


def split3(x):
    high = x.astype(BF16)
    rest = x - high.astype(F32)
    mid = rest.astype(BF16)
    return high, mid, (rest - mid.astype(F32)).astype(BF16)


def dot32(a, b, dims):
    return lax.dot_general(a, b, (dims, ((), ())), preferred_element_type=F32)


def lane_splat(x, c):
    return jnp.broadcast_to(x[:, c : c + 1], x.shape)


def row_splat(x, r):
    return jnp.broadcast_to(x[r : r + 1, :], x.shape)


def tree_sum(terms):
    while len(terms) > 1:
        terms = [
            terms[i] + terms[i + 1] if i + 1 < len(terms) else terms[i]
            for i in range(0, len(terms), 2)
        ]
    return terms[0]


def factor_block(d_ref, w_ref):
    tiles = BLK // SUB
    pivots = 2 * SUB
    rid = lax.broadcasted_iota(jnp.int32, (SUB, BLK), 0)
    lid = lax.broadcasted_iota(jnp.int32, (SUB, BLK), 1)
    a = [d_ref[SUB * i : SUB * i + SUB, :] for i in range(tiles)]
    w = [jnp.where(lid == rid + SUB * i, 1.0, 0.0) for i in range(tiles)]
    for first in range(0, tiles, 2):
        lane = SUB * first
        cols = [[lane_splat(a[first + t], lane + c) for t in range(2)] for c in range(pivots)]
        rows_a = [a[first], a[first + 1]]
        rows_w = [w[first], w[first + 1]]
        low_w = [w[first], w[first + 1]]
        inv_pivots = [jnp.zeros((SUB, BLK), F32) for _ in range(2)]
        pivot = row_splat(cols[0][0], 0)
        for k in range(pivots):
            h, r = divmod(k, SUB)
            inv = 1.0 / pivot
            if k + 1 < pivots:
                h1, r1 = divmod(k + 1, SUB)
                off = row_splat(cols[k + 1][h], r)
                pivot = row_splat(cols[k + 1][h1], r1) - (off * off) * inv
            mult = [
                (jnp.where(rid == r, 0.0, cols[k][t]) if t == h else cols[k][t]) * inv
                for t in range(2)
            ]
            below = [jnp.where(rid > r, mult[t], 0.0) if t == h else mult[t] for t in range(2)]
            for j in range(k + 1, pivots):
                line = row_splat(cols[j][h], r)
                cols[j] = [cols[j][t] - mult[t] * line for t in range(2)]
            line_a, line_w, line_l = (row_splat(x[h], r) for x in (rows_a, rows_w, low_w))
            rows_a = [rows_a[t] - mult[t] * line_a for t in range(2)]
            rows_w = [rows_w[t] - mult[t] * line_w for t in range(2)]
            low_w = [low_w[t] - below[t] * line_l if t >= h else low_w[t] for t in range(2)]
            inv_pivots[h] = jnp.where(rid == r, inv, inv_pivots[h])
        for t in range(2):
            rows_a[t] = rows_a[t] * inv_pivots[t]
            rows_w[t] = rows_w[t] * inv_pivots[t]
            at = lane + SUB * t
            w_ref[at : at + SUB, :] = low_w[t] * jnp.sqrt(inv_pivots[t])
        if first + 2 < tiles:
            splat_a = [row_splat(rows_a[c // SUB], c % SUB) for c in range(pivots)]
            splat_w = [row_splat(rows_w[c // SUB], c % SUB) for c in range(pivots)]
            for i in range(first + 2, tiles):
                p = [lane_splat(a[i], lane + c) for c in range(pivots)]
                a[i] = a[i] - tree_sum([p[c] * splat_a[c] for c in range(pivots)])
                w[i] = w[i] - tree_sum([p[c] * splat_w[c] for c in range(pivots)])


def factor(g_ref, w_ref, d_ref, wk_ref, x_ref, y_ref, z_ref, between):
    size = g_ref.shape[0]
    blocks = size // BLK
    depth = 6 * BLK
    w_ref[...] = jnp.zeros_like(w_ref)
    d_ref[...] = g_ref[0:BLK, 0:BLK]

    def left_of(parts):
        high, mid, low = parts
        return [high, high, mid, high, mid, low]

    def right_of(parts):
        high, mid, low = parts
        return [high, mid, high, low, mid, high]

    def rest(k):
        nxt = (k + 1) * BLK
        j = nxt
        while j < size:
            wide = 2 * BLK if j % (2 * BLK) == 0 else BLK
            g_ref[j:, j : j + wide] -= dot32(x_ref[j:, 0:depth], y_ref[j : j + wide, 0:depth], NT)
            j += wide
        w_ref[nxt:, 0:nxt] -= dot32(x_ref[nxt:, 0:depth], z_ref[0:depth, 0:nxt], NN)

    for k in range(blocks):
        factor_block(d_ref, wk_ref)
        if k > 0:
            rest(k - 1)
        if k == 2:
            between()
        lo = k * BLK
        nxt = lo + BLK
        wk = wk_ref[...]
        wk_parts = split3(wk)
        if nxt < size:
            panel = split3(
                dot32(
                    jnp.concatenate(left_of(split3(g_ref[nxt:, lo:nxt])), axis=1),
                    jnp.concatenate(right_of(wk_parts), axis=1),
                    NT,
                )
            )
            x = jnp.concatenate(left_of(panel), axis=1)
            y = jnp.concatenate(right_of(panel), axis=1)
            x_ref[nxt:, 0:depth] = x
            y_ref[nxt:, 0:depth] = y
            d_ref[...] = g_ref[nxt : nxt + BLK, nxt : nxt + BLK] - dot32(x[0:BLK], y[0:BLK], NT)
        if k > 0:
            row = dot32(
                jnp.concatenate(left_of(wk_parts), axis=1),
                jnp.concatenate(right_of(split3(w_ref[lo:nxt, 0:lo])), axis=0),
                NN,
            )
            w_ref[lo:nxt, 0:lo] = row
            if nxt < size:
                z_ref[0:depth, 0:lo] = jnp.concatenate(right_of(split3(row)), axis=0)
        w_ref[lo:nxt, lo:nxt] = wk
        if nxt < size:
            z_ref[0:depth, lo:nxt] = jnp.concatenate(right_of(wk_parts), axis=0)


class Group:
    def __init__(self, axis, n):
        self.axis, self.n = axis, n
        self.me = lax.axis_index(axis)
        self.unsent = []

    def peer(self, t):
        return lax.rem(self.me + t, self.n)

    def source(self, t):
        return lax.rem(self.me + self.n - t, self.n)

    def each(self, fn):
        def step(t, carry):
            fn(t)
            return carry

        lax.fori_loop(1, self.n, step, 0)

    def copy(self, src, dst, sems, t):
        return pltpu.make_async_remote_copy(
            src_ref=src,
            dst_ref=dst,
            send_sem=sems.at[0, t - 1],
            recv_sem=sems.at[1, t - 1],
            device_id={self.axis: self.peer(t)},
            device_id_type=MESH,
        )

    def greet(self, barrier):
        self.each(
            lambda t: pl.semaphore_signal(
                barrier, inc=1, device_id={self.axis: self.peer(t)}, device_id_type=MESH
            )
        )

    def scatter_start(self, stage, recv, sems):
        self.each(lambda t: self.copy(stage.at[self.peer(t)], recv.at[t - 1], sems, t).start())

    def scatter_finish(self, stage, recv, sems, later=True):
        self.each(lambda t: self.copy(stage.at[self.peer(t)], recv.at[t - 1], sems, t).wait_recv())

        def copy(t):
            return self.copy(stage.at[self.peer(t)], recv.at[t - 1], sems, t)

        if later:
            self.unsent.append(copy)
        else:
            self.each(lambda t: copy(t).wait_send())
        return tree_sum([stage[self.me]] + [recv[t] for t in range(self.n - 1)])

    def scatter_sum(self, stage, recv, sems):
        self.scatter_start(stage, recv, sems)
        return self.scatter_finish(stage, recv, sems)

    def gather_start(self, value, out, sems):
        out[self.me] = value
        self.each(lambda t: self.copy(out.at[self.me], out.at[self.me], sems, t).start())

    def gather_finish(self, out, sems):
        def wait(t):
            src = self.source(t)
            self.copy(out.at[src], out.at[src], sems, t).wait_recv()

        self.each(wait)
        self.unsent.append(lambda t: self.copy(out.at[self.me], out.at[self.me], sems, t))

    def finish_sends(self):
        for copy in self.unsent:
            self.each(lambda t: copy(t).wait_send())

    def gather(self, value, out, sems):
        self.gather_start(value, out, sems)
        self.gather_finish(out, sems)


CORES = 2
SUBS = 2
DIST = (4, 3, -3, 2, -2, 1, -1, 0)
PLUS = (0, 1, 3, 5)
MINUS = (0, 2, 4, 6)
GOT_PLUS = (1, 3, 5, 7)
GOT_MINUS = (2, 4, 6, 7)


class Line:
    def __init__(self, n_dp):
        self.zs = n_dp // CORES
        me = lax.axis_index("dp")
        self.z = me // CORES
        self.c = lax.rem(me, CORES)

    def to(self, hop):
        chip = lax.rem(self.z + hop + self.zs, self.zs)
        return {"dp": chip * CORES + self.c}

    def partner(self):
        return {"dp": self.z * CORES + (1 - self.c)}

    def copy(self, src, dst, sems, at, device):
        return pltpu.make_async_remote_copy(
            src_ref=src,
            dst_ref=dst,
            send_sem=sems.at[(0, *at)],
            recv_sem=sems.at[(1, *at)],
            device_id=device,
            device_id_type=MESH,
        )


def halves_sent(way, s, first):
    if s == (0 if first else 3):
        return (way,)
    return (0, 1)


def sketch_gram(line, ready, loaded, meanwhile, a_ref, s_ref, g_ref, p, pair, ring, gat, gpar, pair_sems, ring_sems, gat_sems, gpar_sems):
    half = p.shape[3]
    sub = half // SUBS
    chunk = 2 * CORES * half
    cols = a_ref.shape[1]
    wide = 2 * LANES

    def partial(*chunks):
        for e in chunks:
            loaded(e)
        rows = [
            s_ref[
                pl.ds(
                    pl.multiple_of(lax.rem(line.z + DIST[e] + line.zs, line.zs) * chunk, 16), chunk
                ),
                :,
            ]
            for e in chunks
        ]
        left = jnp.concatenate(rows, axis=0)

        def tile(i, carry):
            at = pl.multiple_of(i * wide, wide)
            prod = dot32(left, a_ref[:, pl.ds(at, wide)], NN)
            for n, e in enumerate(chunks):
                for d in range(2):
                    for c in range(CORES):
                        r = n * chunk + (d * CORES + c) * half
                        p[e, d, c, :, pl.ds(at, wide)] = prod[r : r + half]
            return carry

        lax.fori_loop(0, cols // wide, tile, 0)

    def pair_copy(e, d):
        return line.copy(
            p.at[e, d, 1 - line.c], pair.at[e, d], pair_sems, (e, d), line.partner()
        )

    def pair_send(*chunks):
        for e in chunks:
            for d in range(2):
                pair_copy(e, d).start()

    def piece(ref, q):
        return ref.at[pl.ds(q * sub, sub), :]

    def ring_copy(way, s, d, q):
        e = (PLUS, MINUS)[way][s]
        return line.copy(
            piece(p.at[e, d, line.c], q),
            piece(ring.at[way, s, d], q),
            ring_sems,
            (way, s, d, q),
            line.to((1, -1)[way]),
        )

    def ring_step(s):
        for e in sorted({PLUS[s], MINUS[s]}):
            for d in range(2):
                pair_copy(e, d).wait_recv()
        for q in range(SUBS):
            for turn in range(2):
                for way in range(2):
                    d = (1 - turn, turn)[way]
                    if d not in halves_sent(way, s, True):
                        continue
                    e = (PLUS, MINUS)[way][s]
                    at = pl.ds(q * sub, sub)
                    value = p[e, d, line.c, at, :] + pair[e, d, at, :]
                    if s > 0 and d in halves_sent(way, s - 1, True):
                        ring_copy(way, s - 1, d, q).wait_recv()
                        value = value + ring[way, s - 1, d, at, :]
                    p[e, d, line.c, at, :] = value
                    ring_copy(way, s, d, q).start()

    def gat_copy(way, s, d, q):
        src = (PLUS, MINUS)[way][s]
        dst = (GOT_PLUS, GOT_MINUS)[way][s]
        return line.copy(
            piece(gat.at[src, d], q),
            piece(gat.at[dst, d], q),
            gat_sems,
            (way, s, d, q),
            line.to((1, -1)[way]),
        )

    def gpar_copy(e, d):
        return line.copy(gat.at[e, d], gpar.at[e, d], gpar_sems, (e, d), line.partner())

    def gather_step(s, pieces):
        for q in pieces:
            for d in range(2):
                for way in range(2):
                    if d not in halves_sent(way, s, False):
                        continue
                    gat_copy(way, s, d, q).wait_recv()
                    if s < 3 and d in halves_sent(way, s + 1, False):
                        gat_copy(way, s + 1, d, q).start()
                    if q == SUBS - 1:
                        gpar_copy((GOT_PLUS, GOT_MINUS)[way][s], d).start()

    partial(0)
    ready()
    pair_send(0)
    ring_step(0)
    partial(1, 2)
    pair_send(1, 2)
    ring_step(1)
    partial(3, 4)
    pair_send(3, 4)
    partial(5, 6)
    pair_send(5, 6)
    ring_step(2)
    partial(7)
    pair_send(7)
    g_ref[...] = jnp.zeros_like(g_ref)
    ring_step(3)
    meanwhile()
    for d in range(2):
        pair_copy(7, d).wait_recv()
    for q in range(SUBS):
        for d in range(2):
            at = pl.ds(q * sub, sub)
            value = p[7, d, line.c, at, :] + pair[7, d, at, :]
            for way in range(2):
                ring_copy(way, 3, d, q).wait_recv()
                value = value + ring[way, 3, d, at, :]
            gat[0, d, at, :] = value
            for way in range(2):
                gat_copy(way, 0, d, q).start()
            if q == SUBS - 1:
                gpar_copy(0, d).start()

    def add(e, carry):
        for at, step, pieces in (
            (1, 0, (0, 1)),
            (2, 1, (0,)),
            (3, 1, (1,)),
            (4, 2, (0,)),
            (5, 2, (1,)),
            (6, 3, (0, 1)),
        ):

            @pl.when(e == at)
            def _():
                gather_step(step, pieces)

        for d in range(2):
            gpar_copy(e, d).wait_recv()
        rows = jnp.concatenate([gat[e, 0], gat[e, 1], gpar[e, 0], gpar[e, 1]], axis=0)
        rh, rm, rl = split3(rows)
        th, tm, tl = split3(rows.T)
        for j in range(0, cols, wide):
            high, mid, low = rh[:, j : j + wide], rm[:, j : j + wide], rl[:, j : j + wide]
            g_ref[j:, j : j + wide] += (
                dot32(th[j:], high, NN)
                + (dot32(th[j:], mid, NN) + dot32(tm[j:], high, NN))
                + (dot32(tm[j:], mid, NN) + dot32(th[j:], low, NN) + dot32(tl[j:], high, NN))
            )
        return carry

    lax.fori_loop(0, 8, add, 0)
    for e in range(8):
        for d in range(2):
            pair_copy(e, d).wait_send()
            gpar_copy(e, d).wait_send()
    for s in range(4):
        for way in range(2):
            for q in range(SUBS):
                for d in halves_sent(way, s, True):
                    ring_copy(way, s, d, q).wait_send()
                for d in halves_sent(way, s, False):
                    gat_copy(way, s, d, q).wait_send()


class Chips(Group):
    def __init__(self, line):
        self.axis, self.n, self.me, self.c = "dp", line.zs, line.z, line.c
        self.unsent = []

    def copy(self, src, dst, sems, t):
        return pltpu.make_async_remote_copy(
            src_ref=src,
            dst_ref=dst,
            send_sem=sems.at[0, t - 1],
            recv_sem=sems.at[1, t - 1],
            device_id={"dp": self.peer(t) * CORES + self.c},
            device_id_type=MESH,
        )


def pair_and_chips_sum(line, value, extra, halves, got, stage, recv, out, sems, pair_sems):
    chips = Chips(line)
    part = value.shape[1] // CORES
    for h in range(CORES):
        halves[h, :, 0:part] = value[:, h * part : (h + 1) * part]
        halves[h, :, part:] = extra
    to_other = line.copy(halves.at[1 - line.c], got, pair_sems, (0,), line.partner())
    to_other.start()
    to_other.wait_recv()
    both = halves[line.c] + got[...]
    for d in range(chips.n):
        stage[d] = both[SUB * d : SUB * d + SUB]
    total = chips.scatter_sum(stage, recv, sems.at[0])
    chips.gather(total, out.at[line.c], sems.at[1])
    back = line.copy(out.at[line.c], out.at[line.c], pair_sems, (1,), line.partner())
    back.start()
    back.wait()
    to_other.wait_send()
    chips.finish_sends()
    rows = value.shape[0]
    total = jnp.concatenate(
        [out[h].reshape(rows, part + LANES)[:, 0:part] for h in range(CORES)], axis=1
    )
    return total, out[0].reshape(rows, part + LANES)[:, part:]


def lane_partial(x):
    return tree_sum(
        [x[:, i : i + LANES] * x[:, i : i + LANES] for i in range(0, x.shape[1], LANES)]
    )


def norm_of(lanes):
    return jnp.sqrt(jnp.sum(lanes, axis=1, keepdims=True) + NORM_EPS)


def put_slices(stage, value, extra):
    n, _, wide = stage.shape
    halves = n * SUB // value.shape[0]
    part = value.shape[1] // halves
    for d in range(n):
        r, h = SUB * (d // halves), part * (d % halves)
        stage[d, :, 0:part] = value[r : r + SUB, h : h + part]
        if extra is not None:
            stage[d, :, part:wide] = extra[r : r + SUB, :]


def take_slices(out, k, part):
    n = out.shape[0]
    halves = n * SUB // k
    value = jnp.concatenate(
        [
            jnp.concatenate([out[g * halves + h, :, 0:part] for h in range(halves)], axis=1)
            for g in range(n // halves)
        ],
        axis=0,
    )
    return value


def take_extra(out, k, part):
    n = out.shape[0]
    halves = n * SUB // k
    return jnp.concatenate(
        [out[g * halves, :, part : part + LANES] for g in range(n // halves)], axis=0
    )


def times_exact(x, mat, dims):
    k = x.shape[0]
    both = dot32(jnp.concatenate(split3(x), axis=0), mat, dims)
    return both[0:k] + (both[k : 2 * k] + both[2 * k : 3 * k])


def times_split(x, parts, dims):
    k = x.shape[0]
    high, mid, low = split3(x)
    mh, mm, ml = parts
    a = dot32(jnp.concatenate([high, mid, low], axis=0), mh, dims)
    b = dot32(jnp.concatenate([high, mid], axis=0), mm, dims)
    c = dot32(high, ml, dims)
    return a[0:k] + ((a[k : 2 * k] + b[0:k]) + ((a[2 * k : 3 * k] + b[k : 2 * k]) + c))


def whole_kernel(
    n_dp,
    n_feat,
    a_hbm,
    s_hbm,
    t_ref,
    sol_ref,
    ratio_ref,
    a_ref,
    s_ref,
    load_sems,
    p,
    pair,
    ring,
    gat,
    gpar,
    pair_sems,
    ring_sems,
    gat_sems,
    gpar_sems,
    g_ref,
    w_ref,
    d_ref,
    wk_ref,
    wh,
    wm,
    wl,
    u_ref,
    img_ref,
    d_stage,
    d_recv,
    d_out,
    d_halves,
    d_got,
    d_stage2,
    d_recv2,
    d_out2,
    f_stage,
    f_recv,
    f_out,
    f_stage_b,
    f_recv_b,
    f_out_b,
    f_stage2,
    f_recv2,
    f_stage2_b,
    f_recv2_b,
    small_dp,
    small_feat,
    dp_sems,
    feat_sems,
    chip_sems,
    chip_pair_sems,
):
    dp = Group("dp", n_dp)
    feat = Group("feat", n_feat)
    k, rows = t_ref.shape
    cols = a_ref.shape[1]
    f_halves = n_feat * SUB // k
    part_rows = rows // PARTS
    f_part = part_rows // f_halves
    d_part = cols // (n_dp * SUB // k)

    line = Line(n_dp)
    chunk = s_ref.shape[0] // line.zs

    def load(e):
        at = pl.ds(
            pl.multiple_of(lax.rem(line.z + DIST[e] + line.zs, line.zs) * chunk, 16), chunk
        )
        return pltpu.make_async_copy(s_hbm.at[at, :], s_ref.at[at, :], load_sems.at[e])

    design_load = pltpu.make_async_copy(a_hbm, a_ref, load_sems.at[line.zs])
    load(0).start()
    design_load.start()
    for e in range(1, line.zs):
        load(e).start()

    def loaded(e):
        if e == 0:
            design_load.wait()
        load(e).wait()

    barrier = pltpu.get_barrier_semaphore()
    dp.greet(barrier)
    feat.greet(barrier)
    def preconditioned(vec):
        return times_split(vec, (wh[...], wm[...], wl[...]), NN)

    def adjoint_pre(vec):
        return times_split(vec, (wh[...], wm[...], wl[...]), NT)

    targets = t_ref[...]

    def ready():
        pl.semaphore_wait(barrier, n_dp + n_feat - 2)

    def meanwhile():
        put_slices(d_stage, times_exact(t_ref[...], a_ref[...], NN), lane_partial(t_ref[...]))

    sketch_gram(
        line, ready, loaded, meanwhile, a_ref, s_ref, g_ref, p, pair, ring, gat, gpar,
        pair_sems, ring_sems, gat_sems, gpar_sems,
    )
    dp.scatter_start(d_stage, d_recv, dp_sems.at[0])

    def between():
        total = dp.scatter_finish(d_stage, d_recv, dp_sems.at[0], later=False)
        dp.gather_start(total, d_out, dp_sems.at[1])

    factor(g_ref, w_ref, d_ref, wk_ref, wh, wm, wl, between)
    dp.gather_finish(d_out, dp_sems.at[1])
    h, m, l = split3(w_ref[...])
    wh[...] = h
    wm[...] = m
    wl[...] = l
    adj, squares = take_slices(d_out, k, d_part), take_extra(d_out, k, d_part)
    beta_first = norm_of(squares)
    u_ref[...] = targets / beta_first

    v_raw = adjoint_pre(adj / beta_first)
    y_raw = preconditioned(v_raw)
    def image_start(y, v, stages, recvs, sems):
        for i in range(PARTS):
            at = i * part_rows
            image = times_exact(y, a_ref[at : at + part_rows, :], NT)
            put_slices(stages[i], image, lane_partial(v) if i == 0 else None)
            feat.scatter_start(stages[i], recvs[i], feat_sems.at[sems + i])

    image_start(y_raw, v_raw, (f_stage, f_stage_b), (f_recv, f_recv_b), 0)
    for i, (stage, recv, out) in enumerate(
        ((f_stage, f_recv, f_out), (f_stage_b, f_recv_b, f_out_b))
    ):
        total = feat.scatter_finish(stage, recv, feat_sems.at[i])
        feat.gather_start(total, out, feat_sems.at[PARTS + i])
    feat.gather_finish(f_out, feat_sems.at[PARTS])
    squares = take_extra(f_out, k, f_part)
    alpha = norm_of(squares)
    v = v_raw / alpha
    w = y_raw / alpha
    rho_bar = alpha
    phi_bar = beta_first

    adj = jnp.zeros((k, cols), F32)
    squares = jnp.zeros((k, LANES), F32)
    for i, out in enumerate((f_out, f_out_b)):
        at = i * part_rows
        if i:
            feat.gather_finish(out, feat_sems.at[PARTS + i])
        part = take_slices(out, k, f_part) / alpha - alpha * u_ref[:, at : at + part_rows]
        u_ref[:, at : at + part_rows] = part
        adj = adj + times_exact(part, a_ref[at : at + part_rows, :], NN)
        squares = squares + lane_partial(part)
    adj, squares = pair_and_chips_sum(
        line, adj, squares, d_halves, d_got, d_stage2, d_recv2, d_out2, chip_sems, chip_pair_sems
    )
    beta = norm_of(squares)
    u_ref[...] = u_ref[...] / beta
    rho = jnp.sqrt(rho_bar * rho_bar + beta * beta)
    cosine = rho_bar / rho
    sine = beta / rho
    phi = cosine * phi_bar
    phi_bar = sine * phi_bar
    coords = (phi / rho) * w
    v_raw = adjoint_pre(adj / beta) - beta * v
    y_raw = preconditioned(v_raw)

    image_start(y_raw, v_raw, (f_stage2, f_stage2_b), (f_recv2, f_recv2_b), 2 * PARTS)
    for i in range(PARTS):
        put_slices(img_ref.at[i], u_ref[:, i * part_rows : (i + 1) * part_rows], None)
    total = feat.scatter_finish(f_stage2, f_recv2, feat_sems.at[2 * PARTS])
    squares = total[:, f_part:]
    alpha = norm_of(squares)
    left = lane_partial(total[:, 0:f_part] / alpha - alpha * img_ref[0, feat.me])
    total = feat.scatter_finish(f_stage2_b, f_recv2_b, feat_sems.at[2 * PARTS + 1])
    left = left + lane_partial(total / alpha - alpha * img_ref[1, feat.me])
    dp.gather(left, small_dp, dp_sems.at[2])
    norms = tree_sum([small_dp[i] for i in range(n_dp)])
    feat.gather(jnp.concatenate([norms, squares], axis=1), small_feat, feat_sems.at[3 * PARTS])
    groups = n_feat // f_halves
    norms = jnp.concatenate(
        [
            tree_sum([small_feat[g * f_halves + i, :, 0:LANES] for i in range(f_halves)])
            for g in range(groups)
        ],
        axis=0,
    )
    squares = jnp.concatenate([small_feat[g * f_halves, :, LANES:] for g in range(groups)], axis=0)
    alpha = norm_of(squares)
    theta = sine * alpha
    rho_bar = -cosine * alpha
    w = y_raw / alpha - (theta / rho) * w
    beta = norm_of(norms)
    rho = jnp.sqrt(rho_bar * rho_bar + beta * beta)
    cosine = rho_bar / rho
    sine = beta / rho
    phi = cosine * phi_bar
    phi_bar = sine * phi_bar
    sol_ref[...] = coords + (phi / rho) * w
    ratio_ref[...] = jnp.broadcast_to(phi_bar / beta_first, ratio_ref.shape)
    dp.finish_sends()
    feat.finish_sends()


def whole(design, sketch, targets, n_dp, n_feat):
    rows, cols = design.shape
    k = targets.shape[0]
    zs = n_dp // CORES
    half = sketch.shape[0] // (2 * n_dp)
    d_wide = cols * k // (n_dp * SUB) + LANES
    f_part = rows * k // (n_feat * SUB * PARTS)
    vmem = pl.BlockSpec(memory_space=pltpu.VMEM)
    sems = pltpu.SemaphoreType.DMA
    d_bufs = [
        pltpu.VMEM((n_dp, SUB, d_wide), F32),
        pltpu.VMEM((n_dp - 1, SUB, d_wide), F32),
        pltpu.VMEM((n_dp, SUB, d_wide), F32),
    ]
    f_bufs, f_bufs_b = (
        [
            pltpu.VMEM((n_feat, SUB, wide), F32),
            pltpu.VMEM((n_feat - 1, SUB, wide), F32),
            pltpu.VMEM((n_feat, SUB, wide), F32),
        ]
        for wide in (f_part + LANES, f_part)
    )
    return pl.pallas_call(
        functools.partial(whole_kernel, n_dp, n_feat),
        out_shape=(
            jax.ShapeDtypeStruct((k, cols), F32),
            jax.ShapeDtypeStruct((k, LANES), F32),
        ),
        in_specs=[pl.BlockSpec(memory_space=pl.ANY)] * 2 + [vmem],
        out_specs=(vmem, vmem),
        scratch_shapes=[
            pltpu.VMEM(design.shape, BF16),
            pltpu.VMEM(sketch.shape, BF16),
            sems((zs + 1,)),
            pltpu.VMEM((zs, 2, CORES, half, cols), F32),
            pltpu.VMEM((zs, 2, half, cols), F32),
            pltpu.VMEM((2, 4, 2, half, cols), F32),
            pltpu.VMEM((zs, 2, half, cols), F32),
            pltpu.VMEM((zs, 2, half, cols), F32),
            sems((2, zs, 2)),
            sems((2, 2, 4, 2, SUBS)),
            sems((2, 2, 4, 2, SUBS)),
            sems((2, zs, 2)),
            pltpu.VMEM((cols, cols), F32),
            pltpu.VMEM((cols, cols), F32),
            pltpu.VMEM((BLK, BLK), F32),
            pltpu.VMEM((BLK, BLK), F32),
        ]
        + [pltpu.VMEM((cols, cols), BF16)] * 3
        + [
            pltpu.VMEM((k, rows), F32),
            pltpu.VMEM((PARTS, n_feat, SUB, f_part), F32),
        ]
        + d_bufs
        + [
            pltpu.VMEM((CORES, k, cols // CORES + LANES), F32),
            pltpu.VMEM((k, cols // CORES + LANES), F32),
            pltpu.VMEM((zs, SUB, cols // CORES + LANES), F32),
            pltpu.VMEM((zs - 1, SUB, cols // CORES + LANES), F32),
            pltpu.VMEM((CORES, zs, SUB, cols // CORES + LANES), F32),
        ]
        + f_bufs
        + f_bufs_b
        + f_bufs[:2]
        + f_bufs_b[:2]
        + [
            pltpu.VMEM((n_dp, SUB, LANES), F32),
            pltpu.VMEM((n_feat, SUB, 2 * LANES), F32),
            sems((3, 2, n_dp - 1)),
            sems((3 * PARTS + 1, 2, n_feat - 1)),
            sems((2, 2, zs - 1)),
            sems((2, 2)),
        ],
        compiler_params=pltpu.CompilerParams(
            collective_id=0, has_side_effects=True, vmem_limit_bytes=62 * MIB
        ),
    )(design, sketch, targets)


def body(n_dp, n_feat, design, sketch, targets):
    sol, ratio = whole(design, sketch, targets, n_dp, n_feat)
    return sol, ratio[:, 0]


def solution(mesh):
    return jax.shard_map(
        functools.partial(body, mesh.shape["dp"], mesh.shape["feat"]),
        mesh=mesh,
        in_specs=(P("dp", "feat"), P(None, "dp"), P(None, "dp")),
        out_specs=(P(None, "feat"), P()),
        check_vma=False,
    )
```

```python
import functools

import jax
import jax.numpy as jnp
from jax import lax
from jax.experimental import pallas as pl
from jax.experimental.pallas import tpu as pltpu
from jax.sharding import PartitionSpec as P

NORM_EPS = 1e-06
F32 = jnp.float32
BF16 = jnp.bfloat16
MESH = pl.DeviceIdType.MESH
NN = ((1,), (0,))
NT = ((1,), (1,))
SUB = 8
LANES = 128
BLK = 128
MIB = 2**20
PARTS = 2


def split3(x):
    high = x.astype(BF16)
    rest = x - high.astype(F32)
    mid = rest.astype(BF16)
    return high, mid, (rest - mid.astype(F32)).astype(BF16)


def dot32(a, b, dims):
    return lax.dot_general(a, b, (dims, ((), ())), preferred_element_type=F32)


def lane_splat(x, c):
    return jnp.broadcast_to(x[:, c : c + 1], x.shape)


def row_splat(x, r):
    return jnp.broadcast_to(x[r : r + 1, :], x.shape)


def tree_sum(terms):
    while len(terms) > 1:
        terms = [
            terms[i] + terms[i + 1] if i + 1 < len(terms) else terms[i]
            for i in range(0, len(terms), 2)
        ]
    return terms[0]


def factor_block(d_ref, w_ref):
    tiles = BLK // SUB
    pivots = 2 * SUB
    rid = lax.broadcasted_iota(jnp.int32, (SUB, BLK), 0)
    lid = lax.broadcasted_iota(jnp.int32, (SUB, BLK), 1)
    a = [d_ref[SUB * i : SUB * i + SUB, :] for i in range(tiles)]
    w = [jnp.where(lid == rid + SUB * i, 1.0, 0.0) for i in range(tiles)]
    for first in range(0, tiles, 2):
        lane = SUB * first
        cols = [[lane_splat(a[first + t], lane + c) for t in range(2)] for c in range(pivots)]
        rows_a = [a[first], a[first + 1]]
        rows_w = [w[first], w[first + 1]]
        low_w = [w[first], w[first + 1]]
        inv_pivots = [jnp.zeros((SUB, BLK), F32) for _ in range(2)]
        pivot = row_splat(cols[0][0], 0)
        for k in range(pivots):
            h, r = divmod(k, SUB)
            inv = 1.0 / pivot
            if k + 1 < pivots:
                h1, r1 = divmod(k + 1, SUB)
                off = row_splat(cols[k + 1][h], r)
                pivot = row_splat(cols[k + 1][h1], r1) - (off * off) * inv
            mult = [
                (jnp.where(rid == r, 0.0, cols[k][t]) if t == h else cols[k][t]) * inv
                for t in range(2)
            ]
            below = [jnp.where(rid > r, mult[t], 0.0) if t == h else mult[t] for t in range(2)]
            for j in range(k + 1, pivots):
                line = row_splat(cols[j][h], r)
                cols[j] = [cols[j][t] - mult[t] * line for t in range(2)]
            line_a, line_w, line_l = (row_splat(x[h], r) for x in (rows_a, rows_w, low_w))
            rows_a = [rows_a[t] - mult[t] * line_a for t in range(2)]
            rows_w = [rows_w[t] - mult[t] * line_w for t in range(2)]
            low_w = [low_w[t] - below[t] * line_l if t >= h else low_w[t] for t in range(2)]
            inv_pivots[h] = jnp.where(rid == r, inv, inv_pivots[h])
        for t in range(2):
            rows_a[t] = rows_a[t] * inv_pivots[t]
            rows_w[t] = rows_w[t] * inv_pivots[t]
            at = lane + SUB * t
            w_ref[at : at + SUB, :] = low_w[t] * jnp.sqrt(inv_pivots[t])
        if first + 2 < tiles:
            splat_a = [row_splat(rows_a[c // SUB], c % SUB) for c in range(pivots)]
            splat_w = [row_splat(rows_w[c // SUB], c % SUB) for c in range(pivots)]
            for i in range(first + 2, tiles):
                p = [lane_splat(a[i], lane + c) for c in range(pivots)]
                a[i] = a[i] - tree_sum([p[c] * splat_a[c] for c in range(pivots)])
                w[i] = w[i] - tree_sum([p[c] * splat_w[c] for c in range(pivots)])


def factor(g_ref, w_ref, d_ref, wk_ref, x_ref, y_ref, z_ref, between):
    size = g_ref.shape[0]
    blocks = size // BLK
    depth = 6 * BLK
    w_ref[...] = jnp.zeros_like(w_ref)
    d_ref[...] = g_ref[0:BLK, 0:BLK]

    def left_of(parts):
        high, mid, low = parts
        return [high, high, mid, high, mid, low]

    def right_of(parts):
        high, mid, low = parts
        return [high, mid, high, low, mid, high]

    def rest(k):
        nxt = (k + 1) * BLK
        j = nxt
        while j < size:
            wide = 2 * BLK if j % (2 * BLK) == 0 else BLK
            g_ref[j:, j : j + wide] -= dot32(x_ref[j:, 0:depth], y_ref[j : j + wide, 0:depth], NT)
            j += wide
        w_ref[nxt:, 0:nxt] -= dot32(x_ref[nxt:, 0:depth], z_ref[0:depth, 0:nxt], NN)

    for k in range(blocks):
        factor_block(d_ref, wk_ref)
        if k > 0:
            rest(k - 1)
        if k == 2:
            between()
        lo = k * BLK
        nxt = lo + BLK
        wk = wk_ref[...]
        wk_parts = split3(wk)
        if nxt < size:
            panel = split3(
                dot32(
                    jnp.concatenate(left_of(split3(g_ref[nxt:, lo:nxt])), axis=1),
                    jnp.concatenate(right_of(wk_parts), axis=1),
                    NT,
                )
            )
            x = jnp.concatenate(left_of(panel), axis=1)
            y = jnp.concatenate(right_of(panel), axis=1)
            x_ref[nxt:, 0:depth] = x
            y_ref[nxt:, 0:depth] = y
            d_ref[...] = g_ref[nxt : nxt + BLK, nxt : nxt + BLK] - dot32(x[0:BLK], y[0:BLK], NT)
        if k > 0:
            row = dot32(
                jnp.concatenate(left_of(wk_parts), axis=1),
                jnp.concatenate(right_of(split3(w_ref[lo:nxt, 0:lo])), axis=0),
                NN,
            )
            w_ref[lo:nxt, 0:lo] = row
            if nxt < size:
                z_ref[0:depth, 0:lo] = jnp.concatenate(right_of(split3(row)), axis=0)
        w_ref[lo:nxt, lo:nxt] = wk
        if nxt < size:
            z_ref[0:depth, lo:nxt] = jnp.concatenate(right_of(wk_parts), axis=0)


class Group:
    def __init__(self, axis, n):
        self.axis, self.n = axis, n
        self.me = lax.axis_index(axis)
        self.unsent = []

    def peer(self, t):
        return lax.rem(self.me + t, self.n)

    def source(self, t):
        return lax.rem(self.me + self.n - t, self.n)

    def each(self, fn):
        def step(t, carry):
            fn(t)
            return carry

        lax.fori_loop(1, self.n, step, 0)

    def copy(self, src, dst, sems, t):
        return pltpu.make_async_remote_copy(
            src_ref=src,
            dst_ref=dst,
            send_sem=sems.at[0, t - 1],
            recv_sem=sems.at[1, t - 1],
            device_id={self.axis: self.peer(t)},
            device_id_type=MESH,
        )

    def greet(self, barrier):
        self.each(
            lambda t: pl.semaphore_signal(
                barrier, inc=1, device_id={self.axis: self.peer(t)}, device_id_type=MESH
            )
        )

    def scatter_start(self, stage, recv, sems):
        self.each(lambda t: self.copy(stage.at[self.peer(t)], recv.at[t - 1], sems, t).start())

    def scatter_finish(self, stage, recv, sems, later=True):
        self.each(lambda t: self.copy(stage.at[self.peer(t)], recv.at[t - 1], sems, t).wait_recv())

        def copy(t):
            return self.copy(stage.at[self.peer(t)], recv.at[t - 1], sems, t)

        if later:
            self.unsent.append(copy)
        else:
            self.each(lambda t: copy(t).wait_send())
        return tree_sum([stage[self.me]] + [recv[t] for t in range(self.n - 1)])

    def scatter_sum(self, stage, recv, sems):
        self.scatter_start(stage, recv, sems)
        return self.scatter_finish(stage, recv, sems)

    def gather_start(self, value, out, sems):
        out[self.me] = value
        self.each(lambda t: self.copy(out.at[self.me], out.at[self.me], sems, t).start())

    def gather_finish(self, out, sems):
        def wait(t):
            src = self.source(t)
            self.copy(out.at[src], out.at[src], sems, t).wait_recv()

        self.each(wait)
        self.unsent.append(lambda t: self.copy(out.at[self.me], out.at[self.me], sems, t))

    def finish_sends(self):
        for copy in self.unsent:
            self.each(lambda t: copy(t).wait_send())

    def gather(self, value, out, sems):
        self.gather_start(value, out, sems)
        self.gather_finish(out, sems)


CORES = 2
SUBS = 2
DIST = (4, 3, -3, 2, -2, 1, -1, 0)
PLUS = (0, 1, 3, 5)
MINUS = (0, 2, 4, 6)
GOT_PLUS = (1, 3, 5, 7)
GOT_MINUS = (2, 4, 6, 7)


class Line:
    def __init__(self, n_dp):
        self.zs = n_dp // CORES
        me = lax.axis_index("dp")
        self.z = me // CORES
        self.c = lax.rem(me, CORES)

    def to(self, hop):
        chip = lax.rem(self.z + hop + self.zs, self.zs)
        return {"dp": chip * CORES + self.c}

    def partner(self):
        return {"dp": self.z * CORES + (1 - self.c)}

    def copy(self, src, dst, sems, at, device):
        return pltpu.make_async_remote_copy(
            src_ref=src,
            dst_ref=dst,
            send_sem=sems.at[(0, *at)],
            recv_sem=sems.at[(1, *at)],
            device_id=device,
            device_id_type=MESH,
        )


def halves_sent(way, s, first):
    if s == (0 if first else 3):
        return (way,)
    return (0, 1)


def sketch_gram(line, ready, loaded, meanwhile, a_ref, s_ref, g_ref, p, pair, ring, gat, gpar, pair_sems, ring_sems, gat_sems, gpar_sems):
    half = p.shape[3]
    sub = half // SUBS
    chunk = 2 * CORES * half
    cols = a_ref.shape[1]
    wide = 2 * LANES

    def partial(*chunks):
        for e in chunks:
            loaded(e)
        rows = [
            s_ref[
                pl.ds(
                    pl.multiple_of(lax.rem(line.z + DIST[e] + line.zs, line.zs) * chunk, 16), chunk
                ),
                :,
            ]
            for e in chunks
        ]
        left = jnp.concatenate(rows, axis=0)

        def tile(i, carry):
            at = pl.multiple_of(i * wide, wide)
            prod = dot32(left, a_ref[:, pl.ds(at, wide)], NN)
            for n, e in enumerate(chunks):
                for d in range(2):
                    for c in range(CORES):
                        r = n * chunk + (d * CORES + c) * half
                        p[e, d, c, :, pl.ds(at, wide)] = prod[r : r + half]
            return carry

        lax.fori_loop(0, cols // wide, tile, 0)

    def pair_copy(e, d):
        return line.copy(
            p.at[e, d, 1 - line.c], pair.at[e, d], pair_sems, (e, d), line.partner()
        )

    def pair_send(*chunks):
        for e in chunks:
            for d in range(2):
                pair_copy(e, d).start()

    def piece(ref, q):
        return ref.at[pl.ds(q * sub, sub), :]

    def ring_copy(way, s, d, q):
        e = (PLUS, MINUS)[way][s]
        return line.copy(
            piece(p.at[e, d, line.c], q),
            piece(ring.at[way, s, d], q),
            ring_sems,
            (way, s, d, q),
            line.to((1, -1)[way]),
        )

    def ring_step(s):
        for e in sorted({PLUS[s], MINUS[s]}):
            for d in range(2):
                pair_copy(e, d).wait_recv()
        for q in range(SUBS):
            for turn in range(2):
                for way in range(2):
                    d = (1 - turn, turn)[way]
                    if d not in halves_sent(way, s, True):
                        continue
                    e = (PLUS, MINUS)[way][s]
                    at = pl.ds(q * sub, sub)
                    value = p[e, d, line.c, at, :] + pair[e, d, at, :]
                    if s > 0 and d in halves_sent(way, s - 1, True):
                        ring_copy(way, s - 1, d, q).wait_recv()
                        value = value + ring[way, s - 1, d, at, :]
                    p[e, d, line.c, at, :] = value
                    ring_copy(way, s, d, q).start()

    def gat_copy(way, s, d, q):
        src = (PLUS, MINUS)[way][s]
        dst = (GOT_PLUS, GOT_MINUS)[way][s]
        return line.copy(
            piece(gat.at[src, d], q),
            piece(gat.at[dst, d], q),
            gat_sems,
            (way, s, d, q),
            line.to((1, -1)[way]),
        )

    def gpar_copy(e, d):
        return line.copy(gat.at[e, d], gpar.at[e, d], gpar_sems, (e, d), line.partner())

    def gather_step(s, pieces):
        for q in pieces:
            for d in range(2):
                for way in range(2):
                    if d not in halves_sent(way, s, False):
                        continue
                    gat_copy(way, s, d, q).wait_recv()
                    if s < 3 and d in halves_sent(way, s + 1, False):
                        gat_copy(way, s + 1, d, q).start()
                    if q == SUBS - 1:
                        gpar_copy((GOT_PLUS, GOT_MINUS)[way][s], d).start()

    partial(0)
    ready()
    pair_send(0)
    ring_step(0)
    partial(1, 2)
    pair_send(1, 2)
    ring_step(1)
    partial(3, 4)
    pair_send(3, 4)
    partial(5, 6)
    pair_send(5, 6)
    ring_step(2)
    partial(7)
    pair_send(7)
    g_ref[...] = jnp.zeros_like(g_ref)
    ring_step(3)
    meanwhile()
    for d in range(2):
        pair_copy(7, d).wait_recv()
    for q in range(SUBS):
        for d in range(2):
            at = pl.ds(q * sub, sub)
            value = p[7, d, line.c, at, :] + pair[7, d, at, :]
            for way in range(2):
                ring_copy(way, 3, d, q).wait_recv()
                value = value + ring[way, 3, d, at, :]
            gat[0, d, at, :] = value
            for way in range(2):
                gat_copy(way, 0, d, q).start()
            if q == SUBS - 1:
                gpar_copy(0, d).start()

    def add(e, carry):
        for at, step, pieces in (
            (1, 0, (0, 1)),
            (2, 1, (0,)),
            (3, 1, (1,)),
            (4, 2, (0,)),
            (5, 2, (1,)),
            (6, 3, (0, 1)),
        ):

            @pl.when(e == at)
            def _():
                gather_step(step, pieces)

        for d in range(2):
            gpar_copy(e, d).wait_recv()
        rows = jnp.concatenate([gat[e, 0], gat[e, 1], gpar[e, 0], gpar[e, 1]], axis=0)
        rh, rm, rl = split3(rows)
        th, tm, tl = split3(rows.T)
        for j in range(0, cols, wide):
            high, mid, low = rh[:, j : j + wide], rm[:, j : j + wide], rl[:, j : j + wide]
            g_ref[j:, j : j + wide] += (
                dot32(th[j:], high, NN)
                + (dot32(th[j:], mid, NN) + dot32(tm[j:], high, NN))
                + (dot32(tm[j:], mid, NN) + dot32(th[j:], low, NN) + dot32(tl[j:], high, NN))
            )
        return carry

    lax.fori_loop(0, 8, add, 0)
    for e in range(8):
        for d in range(2):
            pair_copy(e, d).wait_send()
            gpar_copy(e, d).wait_send()
    for s in range(4):
        for way in range(2):
            for q in range(SUBS):
                for d in halves_sent(way, s, True):
                    ring_copy(way, s, d, q).wait_send()
                for d in halves_sent(way, s, False):
                    gat_copy(way, s, d, q).wait_send()


class Chips(Group):
    def __init__(self, line):
        self.axis, self.n, self.me, self.c = "dp", line.zs, line.z, line.c
        self.unsent = []

    def copy(self, src, dst, sems, t):
        return pltpu.make_async_remote_copy(
            src_ref=src,
            dst_ref=dst,
            send_sem=sems.at[0, t - 1],
            recv_sem=sems.at[1, t - 1],
            device_id={"dp": self.peer(t) * CORES + self.c},
            device_id_type=MESH,
        )


def pair_and_chips_sum(line, value, extra, halves, got, stage, recv, out, sems, pair_sems):
    chips = Chips(line)
    part = value.shape[1] // CORES
    for h in range(CORES):
        halves[h, :, 0:part] = value[:, h * part : (h + 1) * part]
        halves[h, :, part:] = extra
    to_other = line.copy(halves.at[1 - line.c], got, pair_sems, (0,), line.partner())
    to_other.start()
    to_other.wait_recv()
    both = halves[line.c] + got[...]
    for d in range(chips.n):
        stage[d] = both[SUB * d : SUB * d + SUB]
    total = chips.scatter_sum(stage, recv, sems.at[0])
    chips.gather(total, out.at[line.c], sems.at[1])
    back = line.copy(out.at[line.c], out.at[line.c], pair_sems, (1,), line.partner())
    back.start()
    back.wait()
    to_other.wait_send()
    chips.finish_sends()
    rows = value.shape[0]
    total = jnp.concatenate(
        [out[h].reshape(rows, part + LANES)[:, 0:part] for h in range(CORES)], axis=1
    )
    return total, out[0].reshape(rows, part + LANES)[:, part:]


def lane_partial(x):
    return tree_sum(
        [x[:, i : i + LANES] * x[:, i : i + LANES] for i in range(0, x.shape[1], LANES)]
    )


def norm_of(lanes):
    return jnp.sqrt(jnp.sum(lanes, axis=1, keepdims=True) + NORM_EPS)


def put_slices(stage, value, extra):
    n, _, wide = stage.shape
    halves = n * SUB // value.shape[0]
    part = value.shape[1] // halves
    for d in range(n):
        r, h = SUB * (d // halves), part * (d % halves)
        stage[d, :, 0:part] = value[r : r + SUB, h : h + part]
        if extra is not None:
            stage[d, :, part:wide] = extra[r : r + SUB, :]


def take_slices(out, k, part):
    n = out.shape[0]
    halves = n * SUB // k
    value = jnp.concatenate(
        [
            jnp.concatenate([out[g * halves + h, :, 0:part] for h in range(halves)], axis=1)
            for g in range(n // halves)
        ],
        axis=0,
    )
    return value


def take_extra(out, k, part):
    n = out.shape[0]
    halves = n * SUB // k
    return jnp.concatenate(
        [out[g * halves, :, part : part + LANES] for g in range(n // halves)], axis=0
    )


def times_exact(x, mat, dims):
    k = x.shape[0]
    both = dot32(jnp.concatenate(split3(x), axis=0), mat, dims)
    return both[0:k] + (both[k : 2 * k] + both[2 * k : 3 * k])


def times_lower(x, parts, transposed):
    k, size = x.shape
    high, mid, low = split3(x)
    left = jnp.concatenate([high, mid, low], axis=0)
    wide = 2 * BLK
    out = []
    for at in range(0, size, wide):
        end = at + wide
        if transposed:
            lhs, dims = left[:, 0:end], NT
            mh, mm, ml = (p[at:end, 0:end] for p in parts)
        else:
            lhs, dims = left[:, at:], NN
            mh, mm, ml = (p[at:, at:end] for p in parts)
        a = dot32(lhs, mh, dims)
        b = dot32(lhs[0 : 2 * k], mm, dims)
        c = dot32(lhs[0:k], ml, dims)
        out.append(a[0:k] + ((a[k : 2 * k] + b[0:k]) + ((a[2 * k : 3 * k] + b[k : 2 * k]) + c)))
    return jnp.concatenate(out, axis=1)


def whole_kernel(
    n_dp,
    n_feat,
    a_hbm,
    s_hbm,
    t_ref,
    sol_ref,
    ratio_ref,
    a_ref,
    s_ref,
    load_sems,
    p,
    pair,
    ring,
    gat,
    gpar,
    pair_sems,
    ring_sems,
    gat_sems,
    gpar_sems,
    g_ref,
    w_ref,
    d_ref,
    wk_ref,
    wh,
    wm,
    wl,
    u_ref,
    img_ref,
    d_stage,
    d_recv,
    d_out,
    d_halves,
    d_got,
    d_stage2,
    d_recv2,
    d_out2,
    f_stage,
    f_recv,
    f_out,
    f_stage_b,
    f_recv_b,
    f_out_b,
    f_stage2,
    f_recv2,
    f_stage2_b,
    f_recv2_b,
    small_dp,
    small_feat,
    dp_sems,
    feat_sems,
    chip_sems,
    chip_pair_sems,
):
    dp = Group("dp", n_dp)
    feat = Group("feat", n_feat)
    k, rows = t_ref.shape
    cols = a_ref.shape[1]
    f_halves = n_feat * SUB // k
    part_rows = rows // PARTS
    f_part = part_rows // f_halves
    d_part = cols // (n_dp * SUB // k)

    line = Line(n_dp)
    chunk = s_ref.shape[0] // line.zs

    def load(e):
        at = pl.ds(
            pl.multiple_of(lax.rem(line.z + DIST[e] + line.zs, line.zs) * chunk, 16), chunk
        )
        return pltpu.make_async_copy(s_hbm.at[at, :], s_ref.at[at, :], load_sems.at[e])

    design_load = pltpu.make_async_copy(a_hbm, a_ref, load_sems.at[line.zs])
    load(0).start()
    design_load.start()
    for e in range(1, line.zs):
        load(e).start()

    def loaded(e):
        if e == 0:
            design_load.wait()
        load(e).wait()

    barrier = pltpu.get_barrier_semaphore()
    dp.greet(barrier)
    feat.greet(barrier)
    def preconditioned(vec):
        return times_lower(vec, (wh, wm, wl), False)

    def adjoint_pre(vec):
        return times_lower(vec, (wh, wm, wl), True)

    targets = t_ref[...]

    def ready():
        pl.semaphore_wait(barrier, n_dp + n_feat - 2)

    def meanwhile():
        put_slices(d_stage, times_exact(t_ref[...], a_ref[...], NN), lane_partial(t_ref[...]))

    sketch_gram(
        line, ready, loaded, meanwhile, a_ref, s_ref, g_ref, p, pair, ring, gat, gpar,
        pair_sems, ring_sems, gat_sems, gpar_sems,
    )
    dp.scatter_start(d_stage, d_recv, dp_sems.at[0])

    def between():
        total = dp.scatter_finish(d_stage, d_recv, dp_sems.at[0], later=False)
        dp.gather_start(total, d_out, dp_sems.at[1])

    factor(g_ref, w_ref, d_ref, wk_ref, wh, wm, wl, between)
    dp.gather_finish(d_out, dp_sems.at[1])
    for at in range(0, cols, 2 * BLK):
        end = at + 2 * BLK
        for ref, part in zip((wh, wm, wl), split3(w_ref[at:end, 0:end])):
            ref[at:end, 0:end] = part
    adj, squares = take_slices(d_out, k, d_part), take_extra(d_out, k, d_part)
    beta_first = norm_of(squares)
    u_ref[...] = targets / beta_first

    v_raw = adjoint_pre(adj / beta_first)
    y_raw = preconditioned(v_raw)
    def image_start(y, v, stages, recvs, sems):
        for i in range(PARTS):
            at = i * part_rows
            image = times_exact(y, a_ref[at : at + part_rows, :], NT)
            put_slices(stages[i], image, lane_partial(v) if i == 0 else None)
            feat.scatter_start(stages[i], recvs[i], feat_sems.at[sems + i])

    image_start(y_raw, v_raw, (f_stage, f_stage_b), (f_recv, f_recv_b), 0)
    for i, (stage, recv, out) in enumerate(
        ((f_stage, f_recv, f_out), (f_stage_b, f_recv_b, f_out_b))
    ):
        total = feat.scatter_finish(stage, recv, feat_sems.at[i])
        feat.gather_start(total, out, feat_sems.at[PARTS + i])
    feat.gather_finish(f_out, feat_sems.at[PARTS])
    squares = take_extra(f_out, k, f_part)
    alpha = norm_of(squares)
    v = v_raw / alpha
    w = y_raw / alpha
    rho_bar = alpha
    phi_bar = beta_first

    adj = jnp.zeros((k, cols), F32)
    squares = jnp.zeros((k, LANES), F32)
    for i, out in enumerate((f_out, f_out_b)):
        at = i * part_rows
        if i:
            feat.gather_finish(out, feat_sems.at[PARTS + i])
        part = take_slices(out, k, f_part) / alpha - alpha * u_ref[:, at : at + part_rows]
        u_ref[:, at : at + part_rows] = part
        adj = adj + times_exact(part, a_ref[at : at + part_rows, :], NN)
        squares = squares + lane_partial(part)
    adj, squares = pair_and_chips_sum(
        line, adj, squares, d_halves, d_got, d_stage2, d_recv2, d_out2, chip_sems, chip_pair_sems
    )
    beta = norm_of(squares)
    u_ref[...] = u_ref[...] / beta
    rho = jnp.sqrt(rho_bar * rho_bar + beta * beta)
    cosine = rho_bar / rho
    sine = beta / rho
    phi = cosine * phi_bar
    phi_bar = sine * phi_bar
    coords = (phi / rho) * w
    v_raw = adjoint_pre(adj / beta) - beta * v
    y_raw = preconditioned(v_raw)

    image_start(y_raw, v_raw, (f_stage2, f_stage2_b), (f_recv2, f_recv2_b), 2 * PARTS)
    for i in range(PARTS):
        put_slices(img_ref.at[i], u_ref[:, i * part_rows : (i + 1) * part_rows], None)
    total = feat.scatter_finish(f_stage2, f_recv2, feat_sems.at[2 * PARTS])
    squares = total[:, f_part:]
    alpha = norm_of(squares)
    left = lane_partial(total[:, 0:f_part] / alpha - alpha * img_ref[0, feat.me])
    total = feat.scatter_finish(f_stage2_b, f_recv2_b, feat_sems.at[2 * PARTS + 1])
    left = left + lane_partial(total / alpha - alpha * img_ref[1, feat.me])
    dp.gather(left, small_dp, dp_sems.at[2])
    norms = tree_sum([small_dp[i] for i in range(n_dp)])
    feat.gather(jnp.concatenate([norms, squares], axis=1), small_feat, feat_sems.at[3 * PARTS])
    groups = n_feat // f_halves
    norms = jnp.concatenate(
        [
            tree_sum([small_feat[g * f_halves + i, :, 0:LANES] for i in range(f_halves)])
            for g in range(groups)
        ],
        axis=0,
    )
    squares = jnp.concatenate([small_feat[g * f_halves, :, LANES:] for g in range(groups)], axis=0)
    alpha = norm_of(squares)
    theta = sine * alpha
    rho_bar = -cosine * alpha
    w = y_raw / alpha - (theta / rho) * w
    beta = norm_of(norms)
    rho = jnp.sqrt(rho_bar * rho_bar + beta * beta)
    cosine = rho_bar / rho
    sine = beta / rho
    phi = cosine * phi_bar
    phi_bar = sine * phi_bar
    sol_ref[...] = coords + (phi / rho) * w
    ratio_ref[...] = jnp.broadcast_to(phi_bar / beta_first, ratio_ref.shape)
    dp.finish_sends()
    feat.finish_sends()


def whole(design, sketch, targets, n_dp, n_feat):
    rows, cols = design.shape
    k = targets.shape[0]
    zs = n_dp // CORES
    half = sketch.shape[0] // (2 * n_dp)
    d_wide = cols * k // (n_dp * SUB) + LANES
    f_part = rows * k // (n_feat * SUB * PARTS)
    vmem = pl.BlockSpec(memory_space=pltpu.VMEM)
    sems = pltpu.SemaphoreType.DMA
    d_bufs = [
        pltpu.VMEM((n_dp, SUB, d_wide), F32),
        pltpu.VMEM((n_dp - 1, SUB, d_wide), F32),
        pltpu.VMEM((n_dp, SUB, d_wide), F32),
    ]
    f_bufs, f_bufs_b = (
        [
            pltpu.VMEM((n_feat, SUB, wide), F32),
            pltpu.VMEM((n_feat - 1, SUB, wide), F32),
            pltpu.VMEM((n_feat, SUB, wide), F32),
        ]
        for wide in (f_part + LANES, f_part)
    )
    return pl.pallas_call(
        functools.partial(whole_kernel, n_dp, n_feat),
        out_shape=(
            jax.ShapeDtypeStruct((k, cols), F32),
            jax.ShapeDtypeStruct((k, LANES), F32),
        ),
        in_specs=[pl.BlockSpec(memory_space=pl.ANY)] * 2 + [vmem],
        out_specs=(vmem, vmem),
        scratch_shapes=[
            pltpu.VMEM(design.shape, BF16),
            pltpu.VMEM(sketch.shape, BF16),
            sems((zs + 1,)),
            pltpu.VMEM((zs, 2, CORES, half, cols), F32),
            pltpu.VMEM((zs, 2, half, cols), F32),
            pltpu.VMEM((2, 4, 2, half, cols), F32),
            pltpu.VMEM((zs, 2, half, cols), F32),
            pltpu.VMEM((zs, 2, half, cols), F32),
            sems((2, zs, 2)),
            sems((2, 2, 4, 2, SUBS)),
            sems((2, 2, 4, 2, SUBS)),
            sems((2, zs, 2)),
            pltpu.VMEM((cols, cols), F32),
            pltpu.VMEM((cols, cols), F32),
            pltpu.VMEM((BLK, BLK), F32),
            pltpu.VMEM((BLK, BLK), F32),
        ]
        + [pltpu.VMEM((cols, cols), BF16)] * 3
        + [
            pltpu.VMEM((k, rows), F32),
            pltpu.VMEM((PARTS, n_feat, SUB, f_part), F32),
        ]
        + d_bufs
        + [
            pltpu.VMEM((CORES, k, cols // CORES + LANES), F32),
            pltpu.VMEM((k, cols // CORES + LANES), F32),
            pltpu.VMEM((zs, SUB, cols // CORES + LANES), F32),
            pltpu.VMEM((zs - 1, SUB, cols // CORES + LANES), F32),
            pltpu.VMEM((CORES, zs, SUB, cols // CORES + LANES), F32),
        ]
        + f_bufs
        + f_bufs_b
        + f_bufs[:2]
        + f_bufs_b[:2]
        + [
            pltpu.VMEM((n_dp, SUB, LANES), F32),
            pltpu.VMEM((n_feat, SUB, 2 * LANES), F32),
            sems((3, 2, n_dp - 1)),
            sems((3 * PARTS + 1, 2, n_feat - 1)),
            sems((2, 2, zs - 1)),
            sems((2, 2)),
        ],
        compiler_params=pltpu.CompilerParams(
            collective_id=0, has_side_effects=True, vmem_limit_bytes=62 * MIB
        ),
    )(design, sketch, targets)


def body(n_dp, n_feat, design, sketch, targets):
    sol, ratio = whole(design, sketch, targets, n_dp, n_feat)
    return sol, ratio[:, 0]


def solution(mesh):
    return jax.shard_map(
        functools.partial(body, mesh.shape["dp"], mesh.shape["feat"]),
        mesh=mesh,
        in_specs=(P("dp", "feat"), P(None, "dp"), P(None, "dp")),
        out_specs=(P(None, "feat"), P()),
        check_vma=False,
    )
```
